256 devices in a mesh: trade: 8 (over x, y_lo), path: 32 (over y_hi, z, core).
Axes of the slice: x: 4, y: 4 (y_hi: 2, y_lo: 2; y = y_hi * 2 + y_lo), z: 8, core: 2. Of those that a mesh axis runs over, the one named last changes fastest.
Arguments:
- coef: float32 [4, 16, 32768], P(None, None, 'trade'), may hold values from -1.5 to 1.5
- set_ids: int32 [32768], P('trade'), may hold values from 0 to 63
- bucket_ids: int32 [32768], P('trade'), may hold values from 0 to 599
- states: int32 [4, 64], P(None, 'path'), may hold values from 0 to 127
- table: float32 [4, 16, 128], replicated, may hold values from -6 to 6
- risk_weight: float32 [600], replicated, may hold values from 1 to 10
- correlation: float32 [600, 600], replicated, may hold values from 0 to 1, as said below
- date_weight: float32 [4], replicated, may hold values from 0.5 to 1.5
Outputs:
- coef_grad: float32 [4, 16, 32768], P(None, None, ('trade', 'path'))
The draws below stay inside these ranges and needn't reach their ends.
Inputs may be any that keep to these rules, and one draw needn't show every extreme that they name: `correlation`: symmetric and positive definite with unit diagonal.
All inputs are finite; a program needn't handle non-finite values.
Results may differ from the reference program's by a relative error of at most 0.0022.
Values may be sent and summed in bfloat16 or wider, within the bound.
A program may use at most 64 MiB of HBM per device.

```python
import math
import jax
import jax.numpy as jnp
import numpy as np
from jax import lax

NB = 600
K = 16
DATES = 4
NSTATE = 128
TRADES = 32768
PATHS = 64
NSET = 64


def draw_correlation(key, part):
    key = jax.random.fold_in(key, 7)
    keys = jax.random.split(key, 4)
    groups = jax.random.randint(keys[0], (NB,), 0, 20)
    global_load = jax.random.uniform(keys[1], (NB,), jnp.float32, 0.3, 0.55)
    block_load = jax.random.uniform(keys[2], (NB,), jnp.float32, 0.4, 0.75)
    places = jax.random.uniform(keys[3], (NB,), jnp.float32, 0.0, 1.0) * NB
    same_group = (groups[:, None] == groups[None, :]).astype(jnp.float32)
    factor = global_load[:, None] * global_load[None, :] + same_group * block_load[:, None] * block_load[None, :]
    kernel = jnp.exp(-jnp.abs(places[:, None] - places[None, :]) / 15.0)
    eye_mat = jnp.eye(NB, dtype=jnp.float32)
    mixed = 0.7 * factor + 0.3 * kernel
    return mixed * (1.0 - eye_mat) + eye_mat


def place_ends(values, own_key, low, high):
    longest = values.shape.index(max(values.shape))
    spots = []
    for shift in (0, 1):
        where = [jax.random.randint(jax.random.fold_in(own_key, axis), (), 0, length) for axis, length in enumerate(values.shape)]
        where[longest] = (where[longest] + shift) % values.shape[longest]
        spots.append(tuple(where))
    return values.at[spots[0]].set(low).at[spots[1]].set(high)


def level_of(own_key, dims, cuts, smallest, largest):
    def one(dim, parts):
        steps = jax.random.uniform(jax.random.fold_in(jax.random.fold_in(own_key, 6), dim), (parts,), jnp.float32, smallest / len(cuts), largest / len(cuts))
        return jnp.repeat(jnp.exp(steps), dims[dim] // parts).reshape((-1,) + (1,) * (len(dims) - dim - 1))

    level = one(*cuts[0])
    for cut in cuts[1:]:
        level = level * one(*cut)
    return level


def rank_table(count, slope):
    weights = [(1 << 20) // math.isqrt(grade ** slope) + 1 for grade in range(1, count + 1)]
    scale = 1 + sum(weights) // (1 << 30)
    return np.cumsum(np.array([max(1, weight // scale) for weight in weights]))


def ranked(own_key, extent, amount, lean):
    table = rank_table(amount, lean)
    pick = jax.random.randint(jax.random.fold_in(own_key, 1), extent, 0, int(table[amount - 1]))
    standing = jnp.searchsorted(jnp.asarray(table, jnp.int32), pick, side="right")
    return jax.random.permutation(jax.random.fold_in(own_key, 2), amount)[standing].astype(jnp.int32)


def gaussian(key, shape, deviation, reach, cuts=(), kind=jnp.bfloat16):
    array = deviation * jax.random.normal(key, shape, jnp.float32)
    if cuts:
        array = array * level_of(key, shape, cuts, -0.22, 0.18)
    return jnp.clip(array, -reach, reach).astype(kind)


def setup_inputs(seed: int = 0) -> dict:
    seeds = jax.random.split(jax.random.key(seed), 9)
    coef = gaussian(seeds[0], (DATES, K, TRADES), K ** -0.5, 1.5, ((2, 8),), jnp.float32)
    set_ids = place_ends(ranked(seeds[1], (TRADES,), NSET, 2), jax.random.fold_in(seeds[1], 3), 0, NSET - 1).astype(jnp.int32)
    bucket_ids = place_ends(ranked(seeds[2], (TRADES,), NB, 1), jax.random.fold_in(seeds[2], 3), 0, NB - 1).astype(jnp.int32)
    states = place_ends(jax.random.randint(seeds[3], (DATES, PATHS), 0, NSTATE), jax.random.fold_in(seeds[3], 1), 0, NSTATE - 1).astype(jnp.int32)
    table = gaussian(seeds[4], (DATES, K, NSTATE), 1.0, 6.0, (), jnp.float32)
    risk_weight = jnp.clip(jnp.exp(jax.random.uniform(seeds[5], (NB,), jnp.float32, math.log(1.0), math.log(10.0))), 1.0, 10.0)
    correlation = draw_correlation(jax.random.fold_in(seeds[8], 71), 0)
    date_weight = jnp.clip(jax.random.uniform(seeds[7], (DATES,), jnp.float32, 0.5, 1.5), 0.5, 1.5)
    return {"coef": coef, "set_ids": set_ids, "bucket_ids": bucket_ids, "states": states, "table": table, "risk_weight": risk_weight, "correlation": correlation, "date_weight": date_weight}


def reference(coef, set_ids, bucket_ids, states, table, risk_weight, correlation, date_weight):
    cells = set_ids * NB + bucket_ids
    results = []
    for date in range(DATES):
        basis = jnp.take(table[date], states[date], axis=1).T
        sens = jnp.dot(basis, coef[date], precision=lax.Precision.HIGHEST).astype(jnp.bfloat16)
        sens = lax.optimization_barrier(sens).astype(jnp.float32)
        summed = jax.ops.segment_sum(sens.T, cells, num_segments=NSET * NB)
        netted = summed.reshape(NSET, NB, PATHS).transpose(0, 2, 1)
        weighted = netted * risk_weight
        corr_weighted = jnp.dot(weighted.reshape(-1, NB), correlation, precision=lax.Precision.HIGHEST).reshape(netted.shape)
        margin = jnp.sqrt(lax.optimization_barrier(jnp.sum(weighted * corr_weighted, axis=-1)) + 1.0)
        net_grad = (date_weight[date] * risk_weight * corr_weighted / margin[..., None]).astype(jnp.bfloat16)
        net_grad = lax.optimization_barrier(net_grad).astype(jnp.float32)
        picked = net_grad.transpose(0, 2, 1).reshape(NSET * NB, PATHS)[cells]
        results.append(jnp.dot(basis.T, picked.T, precision=lax.Precision.HIGHEST))
    return jnp.stack(results)
```

```python
import functools

import jax
import jax.numpy as jnp
from jax import lax
from jax.experimental import pallas as pl
from jax.experimental.pallas import tpu as pltpu
from jax.sharding import PartitionSpec as P

DATES = 4
SETS = 64
LO = 256
GROUPS = 3
HI = GROUPS * SETS
LANES = 128
MESH = pl.DeviceIdType.MESH
BF = jnp.bfloat16
F32 = jnp.float32
NT = (((1,), (1,)), ((), ()))


def split3(x):
    a = x.astype(BF)
    r = x - a.astype(F32)
    b = r.astype(BF)
    c = (r - b.astype(F32)).astype(BF)
    return a, b, c


def kernel(
    nt,
    npath,
    coef_ref,
    set_ref,
    bkt_ref,
    st_ref,
    table_ref,
    rw_ref,
    corr_ref,
    dw_ref,
    out_ref,
    part,
    sens_out,
    sens_in,
    cell_in,
    hi_f,
    lo_f,
    s_f,
    acc,
    chi,
    clo,
    grad,
    tgp,
    tg,
    tg_in,
    tgx,
    pr,
    st_out,
    st_in,
    sens_ss,
    sens_rs,
    cell_ss,
    cell_rs,
    tg_ss,
    tg_rs,
    st_ss,
    st_rs,
    pr_ss,
    pr_rs,
):
    me = lax.axis_index("trade")
    mp = lax.axis_index("path")
    rows = set_ref.shape[0]
    nb = corr_ref.shape[0]

    barrier = pltpu.get_barrier_semaphore()
    for r in range(1, nt):
        pl.semaphore_signal(
            barrier, inc=1, device_id={"trade": lax.rem(me + r, nt)}, device_id_type=MESH
        )

    def greet(r, c):
        pl.semaphore_signal(
            barrier, inc=1, device_id={"path": lax.rem(mp + r, npath)}, device_id_type=MESH
        )
        return c

    lax.fori_loop(1, npath, greet, 0)

    bkt = bkt_ref[...]
    group = (bkt >= LO).astype(jnp.int32) + (bkt >= 2 * LO).astype(jnp.int32)
    hi = group * SETS + set_ref[...]
    lo = bkt - group * LO
    cell_in[me] = hi * LO + lo

    lane = lax.broadcasted_iota(jnp.int32, table_ref.shape[1:], 1)
    for d in range(DATES):
        for p in range(nt // DATES):
            q = d * (nt // DATES) + p
            state = st_ref[d, p]
            st_out[q : q + 1, :] = jnp.full((1, LANES), state, jnp.int32).astype(F32)
            col = jnp.sum(
                jnp.where(lane == state, table_ref[d], 0.0), axis=1, keepdims=True
            )
            for c in range(rows):
                x = coef_ref[d, :, c * LANES : (c + 1) * LANES] * col
                part[c * 8 : (c + 1) * 8, :] = x[:8] + x[8:]
            for g in range(rows // 8):
                tot = part[pl.ds(g * 64, 8, stride=8), :]
                for s in range(1, 8):
                    tot = tot + part[pl.ds(g * 64 + s, 8, stride=8), :]
                s_f[g * 8 : (g + 1) * 8, :] = tot
            sens_out[q] = s_f[0:rows, :].astype(BF)

    pl.semaphore_wait(barrier, nt - 1 + npath - 1)

    def trade_copies(r):
        peer = lax.rem(me + r, nt)
        return (
            pltpu.make_async_remote_copy(
                src_ref=cell_in.at[me],
                dst_ref=cell_in.at[me],
                send_sem=cell_ss.at[r],
                recv_sem=cell_rs.at[r],
                device_id={"trade": peer},
                device_id_type=MESH,
            ),
            pltpu.make_async_remote_copy(
                src_ref=sens_out.at[peer],
                dst_ref=sens_in.at[me],
                send_sem=sens_ss.at[r],
                recv_sem=sens_rs.at[r],
                device_id={"trade": peer},
                device_id_type=MESH,
            ),
        )

    for r in range(1, nt):
        for copy in trade_copies(r):
            copy.start()
    sens_in[me] = sens_out[me]

    def send_state(r, c):
        pltpu.make_async_remote_copy(
            src_ref=st_out,
            dst_ref=st_in.at[mp],
            send_sem=st_ss,
            recv_sem=st_rs,
            device_id={"path": lax.rem(mp + r, npath)},
            device_id_type=MESH,
        ).start()
        return c

    lax.fori_loop(1, npath, send_state, 0)
    st_in[mp] = st_out[...]

    chi[...] = jnp.zeros_like(chi)
    clo[...] = jnp.zeros_like(clo)
    corr = corr_ref[...]
    top = corr.astype(BF)
    chi[0:nb, 0:nb] = top
    clo[0:nb, 0:nb] = (corr - top.astype(F32)).astype(BF)

    acc[...] = jnp.zeros_like(acc)
    hi_iota = lax.broadcasted_iota(jnp.int32, (HI, LANES), 0).astype(F32).astype(BF)
    lo_iota = lax.broadcasted_iota(jnp.int32, (LO, LANES), 0).astype(F32).astype(BF)
    one, zero = jnp.ones((), BF), jnp.zeros((), BF)

    def spread(ref, row, n):
        x = jnp.broadcast_to(ref[pl.ds(row, 1), :], (16, LANES)).astype(BF)
        return jnp.broadcast_to(x[None], (n // 16, 16, LANES)).reshape(n, LANES)

    def bucket_hot(row):
        return jnp.where(spread(lo_f, row, LO) == lo_iota, one, zero)

    def set_hot(row):
        return jnp.where(spread(hi_f, row, HI) == hi_iota, spread(s_f, row, HI), zero)

    def net_block(src):
        base = pl.multiple_of(src * rows, rows)
        cells = cell_in[src]
        h = lax.shift_right_logical(cells, 8)
        hi_f[pl.ds(base, rows), :] = h.astype(F32)
        lo_f[pl.ds(base, rows), :] = (cells - h * LO).astype(F32)
        s_f[pl.ds(base, rows), :] = sens_in[src].astype(F32)

        def step(g, c):
            row = base + g * 8
            left = jnp.concatenate([set_hot(row + i) for i in range(8)], axis=1)
            right = jnp.concatenate([bucket_hot(row + i) for i in range(8)], axis=1)
            acc[...] += lax.dot_general(left, right, NT, preferred_element_type=F32)
            return c

        lax.fori_loop(0, rows // 8, step, 0)

    net_block(me)

    def net_from(r, c):
        for copy in trade_copies(r):
            copy.wait_recv()
        net_block(lax.rem(me + nt - r, nt))
        return c

    lax.fori_loop(1, nt, net_from, 0)

    rw = rw_ref[...]
    weighted = [acc[g * SETS : (g + 1) * SETS, :] * rw[:, g * LO : (g + 1) * LO] for g in range(GROUPS)]
    w = jnp.concatenate(weighted, axis=1)
    w_hi = w.astype(BF)
    w_lo = (w - w_hi.astype(F32)).astype(BF)
    cw = (
        jnp.dot(w_hi, chi[...], preferred_element_type=F32)
        + jnp.dot(w_hi, clo[...], preferred_element_type=F32)
        + jnp.dot(w_lo, chi[...], preferred_element_type=F32)
    )
    margin = jnp.sqrt(jnp.sum(w * cw, axis=1, keepdims=True) + 1.0)
    weight = dw_ref[me // (nt // DATES)]
    net_grad = ((weight * rw) * cw / margin).astype(BF)
    for g in range(GROUPS):
        grad[g * SETS : (g + 1) * SETS, :] = net_grad[:, g * LO : (g + 1) * LO]

    hi_iota8 = lax.broadcasted_iota(jnp.int32, (HI, LANES), 0).astype(F32)

    def pick_block(dst):
        base = pl.multiple_of(dst * rows, rows)

        def step(g, c):
            row = pl.multiple_of(base + g * 8, 8)
            right = jnp.concatenate([bucket_hot(row + i) for i in range(8)], axis=1)
            product = jnp.dot(grad[...], right, preferred_element_type=F32)
            for i in range(8):
                h = jnp.broadcast_to(hi_f[pl.ds(row + i, 1), :], (HI, LANES))
                kept = jnp.where(h == hi_iota8, product[:, i * LANES : (i + 1) * LANES], 0.0)
                tgp[i * 8 : (i + 1) * 8, :] = jnp.sum(kept.reshape(HI // 8, 8, LANES), axis=0)
            tot = tgp[pl.ds(0, 8, stride=8), :]
            for s in range(1, 8):
                tot = tot + tgp[pl.ds(s, 8, stride=8), :]
            tg[pl.ds(row, 8), :] = tot
            return c

        lax.fori_loop(0, rows // 8, step, 0)

    def pick_copy(r):
        peer = lax.rem(me + r, nt)
        return pltpu.make_async_remote_copy(
            src_ref=tg.at[pl.ds(pl.multiple_of(peer * rows, rows), rows)],
            dst_ref=tg_in.at[pl.ds(pl.multiple_of(me * rows, rows), rows)],
            send_sem=tg_ss.at[r],
            recv_sem=tg_rs.at[r],
            device_id={"trade": peer},
            device_id_type=MESH,
        )

    def pick_to(r, c):
        pick_block(lax.rem(me + r, nt))
        pick_copy(r).start()
        return c

    lax.fori_loop(1, nt, pick_to, 0)
    pick_block(me)
    own = pl.ds(pl.multiple_of(me * rows, rows), rows)
    tg_in[own, :] = tg[own, :]
    for r in range(1, nt):
        pick_copy(r).wait_recv()

    for c in range(rows):
        tgx[c] = tg_in[pl.ds(c, nt, stride=rows), :]

    def send_grad(r, c):
        peer = lax.rem(mp + r, npath)
        pltpu.make_async_remote_copy(
            src_ref=tgx.at[peer],
            dst_ref=pr.at[mp],
            send_sem=pr_ss,
            recv_sem=pr_rs,
            device_id={"path": peer},
            device_id_type=MESH,
        ).start()
        return c

    lax.fori_loop(1, npath, send_grad, 0)
    pr[mp] = tgx[mp]

    others = pl.ds(0, npath - 1)
    pltpu.make_async_copy(st_in.at[others], st_in.at[others], st_rs).wait()
    pairs = npath * nt
    ks = table_ref.shape[1]
    states = st_in[...].reshape(pairs, LANES)
    hot = (states == lax.broadcasted_iota(jnp.int32, (pairs, LANES), 1).astype(F32)).astype(F32).astype(BF)
    tab = table_ref[...].reshape(DATES * ks, LANES)
    at_date = lax.broadcasted_iota(jnp.int32, (DATES * ks, pairs), 0) // ks
    pair_date = (lax.broadcasted_iota(jnp.int32, (DATES * ks, pairs), 1) % nt) // (nt // DATES)
    basis = [
        jnp.where(
            at_date == pair_date, lax.dot_general(t, hot, NT, preferred_element_type=F32), 0.0
        ).astype(BF)
        for t in split3(tab)
    ]

    pltpu.make_async_copy(pr.at[others], pr.at[others], pr_rs).wait()
    right = pr[...].reshape(pairs, LANES).astype(BF)
    total = jnp.dot(basis[0], right, preferred_element_type=F32)
    for b in basis[1:]:
        total = total + jnp.dot(b, right, preferred_element_type=F32)
    out_ref[...] = total.reshape(DATES, ks, LANES)

    for r in range(1, nt):
        for copy in trade_copies(r):
            copy.wait_send()
        pick_copy(r).wait_send()
    pltpu.make_async_copy(st_in.at[others], st_in.at[others], st_ss).wait()
    pltpu.make_async_copy(pr.at[others], pr.at[others], pr_ss).wait()


def per_device(coef, set_ids, bucket_ids, states, table, risk_weight, correlation, date_weight):
    nt = lax.axis_size("trade")
    npath = lax.axis_size("path")
    trades = coef.shape[2]
    rows = trades // LANES
    nb = correlation.shape[0]
    ks = table.shape[1]
    vmem = pl.BlockSpec(memory_space=pltpu.VMEM)
    smem = pl.BlockSpec(memory_space=pltpu.SMEM)
    rw = jnp.pad(risk_weight, (0, GROUPS * LO - nb)).reshape(1, GROUPS * LO)
    dma = pltpu.SemaphoreType.DMA
    return pl.pallas_call(
        functools.partial(kernel, nt, npath),
        out_shape=jax.ShapeDtypeStruct((DATES, ks, LANES), F32),
        in_specs=[vmem, vmem, vmem, smem, vmem, vmem, vmem, smem],
        out_specs=vmem,
        scratch_shapes=[
            pltpu.VMEM((rows * 8, LANES), F32),
            pltpu.VMEM((nt, rows, LANES), BF),
            pltpu.VMEM((nt, rows, LANES), BF),
            pltpu.VMEM((nt, rows, LANES), jnp.int32),
            pltpu.VMEM((nt * rows, LANES), F32),
            pltpu.VMEM((nt * rows, LANES), F32),
            pltpu.VMEM((nt * rows, LANES), F32),
            pltpu.VMEM((HI, LO), F32),
            pltpu.VMEM((GROUPS * LO, GROUPS * LO), BF),
            pltpu.VMEM((GROUPS * LO, GROUPS * LO), BF),
            pltpu.VMEM((HI, LO), BF),
            pltpu.VMEM((64, LANES), F32),
            pltpu.VMEM((nt * rows, LANES), F32),
            pltpu.VMEM((nt * rows, LANES), F32),
            pltpu.VMEM((npath, nt, LANES), F32),
            pltpu.VMEM((npath, nt, LANES), F32),
            pltpu.VMEM((nt, LANES), F32),
            pltpu.VMEM((npath, nt, LANES), F32),
            dma((nt,)),
            dma((nt,)),
            dma((nt,)),
            dma((nt,)),
            dma((nt,)),
            dma((nt,)),
            dma,
            dma,
            dma,
            dma,
        ],
        compiler_params=pltpu.CompilerParams(
            collective_id=0, has_side_effects=True, vmem_limit_bytes=48 * 1024 * 1024
        ),
    )(
        coef,
        set_ids.reshape(rows, LANES),
        bucket_ids.reshape(rows, LANES),
        states,
        table,
        rw,
        correlation,
        date_weight,
    )


def solution(mesh):
    in_specs = (P(None, None, "trade"), P("trade"), P("trade"), P(None, "path"), P(), P(), P(), P())
    out_specs = P(None, None, ("trade", "path"))
    return jax.shard_map(
        per_device, mesh=mesh, in_specs=in_specs, out_specs=out_specs, check_vma=False
    )
```

```python
import functools

import jax
import jax.numpy as jnp
from jax import lax
from jax.experimental import pallas as pl
from jax.experimental.pallas import tpu as pltpu
from jax.sharding import PartitionSpec as P

DATES = 4
SETS = 64
LO = 256
GROUPS = 3
HI = GROUPS * SETS
LANES = 128
MESH = pl.DeviceIdType.MESH
BF = jnp.bfloat16
F32 = jnp.float32
NT = (((1,), (1,)), ((), ()))


def split3(x):
    a = x.astype(BF)
    r = x - a.astype(F32)
    b = r.astype(BF)
    c = (r - b.astype(F32)).astype(BF)
    return a, b, c


def kernel(
    nt,
    npath,
    coef_hbm,
    set_hbm,
    bkt_hbm,
    st_hbm,
    table_hbm,
    rw_hbm,
    corr_hbm,
    dw_hbm,
    out_ref,
    coef_ref,
    set_ref,
    bkt_ref,
    st_ref,
    table_ref,
    rw_ref,
    corr_ref,
    dw_ref,
    load_sem,
    part,
    sens_out,
    sens_in,
    cell_in,
    hi_f,
    lo_f,
    s_f,
    acc,
    chi,
    clo,
    grad,
    tgp,
    tg,
    tg_in,
    tgx,
    pr,
    st_out,
    st_in,
    sens_ss,
    sens_rs,
    cell_ss,
    cell_rs,
    tg_ss,
    tg_rs,
    st_ss,
    st_rs,
    pr_ss,
    pr_rs,
):
    me = lax.axis_index("trade")
    mp = lax.axis_index("path")
    rows = set_ref.shape[0]
    nb = corr_ref.shape[0]

    loads = [
        pltpu.make_async_copy(src, dst, load_sem.at[i])
        for i, (src, dst) in enumerate(
            (
                (set_hbm, set_ref),
                (bkt_hbm, bkt_ref),
                (st_hbm, st_ref),
                (table_hbm, table_ref),
                (coef_hbm, coef_ref),
                (corr_hbm, corr_ref),
                (rw_hbm, rw_ref),
                (dw_hbm, dw_ref),
            )
        )
    ]
    for load in loads:
        load.start()

    barrier = pltpu.get_barrier_semaphore()
    for r in range(1, nt):
        pl.semaphore_signal(
            barrier, inc=1, device_id={"trade": lax.rem(me + r, nt)}, device_id_type=MESH
        )

    def greet(r, c):
        pl.semaphore_signal(
            barrier, inc=1, device_id={"path": lax.rem(mp + r, npath)}, device_id_type=MESH
        )
        return c

    lax.fori_loop(1, npath, greet, 0)

    loads[0].wait()
    loads[1].wait()
    bkt = bkt_ref[...]
    group = (bkt >= LO).astype(jnp.int32) + (bkt >= 2 * LO).astype(jnp.int32)
    hi = group * SETS + set_ref[...]
    lo = bkt - group * LO
    cell_in[me] = hi * LO + lo

    for load in loads[2:5]:
        load.wait()
    lane = lax.broadcasted_iota(jnp.int32, table_ref.shape[1:], 1)
    for d in range(DATES):
        for p in range(nt // DATES):
            q = d * (nt // DATES) + p
            state = st_ref[p, d]
            st_out[q : q + 1, :] = jnp.full((1, LANES), state, jnp.int32).astype(F32)
            col = jnp.sum(
                jnp.where(lane == state, table_ref[d], 0.0), axis=1, keepdims=True
            )
            for c in range(rows):
                x = coef_ref[d, :, c * LANES : (c + 1) * LANES] * col
                part[c * 8 : (c + 1) * 8, :] = x[:8] + x[8:]
            for g in range(rows // 8):
                tot = part[pl.ds(g * 64, 8, stride=8), :]
                for s in range(1, 8):
                    tot = tot + part[pl.ds(g * 64 + s, 8, stride=8), :]
                s_f[g * 8 : (g + 1) * 8, :] = tot
            sens_out[q] = s_f[0:rows, :].astype(BF)

    pl.semaphore_wait(barrier, nt - 1 + npath - 1)

    def trade_copies(r):
        peer = lax.rem(me + r, nt)
        return (
            pltpu.make_async_remote_copy(
                src_ref=cell_in.at[me],
                dst_ref=cell_in.at[me],
                send_sem=cell_ss.at[r],
                recv_sem=cell_rs.at[r],
                device_id={"trade": peer},
                device_id_type=MESH,
            ),
            pltpu.make_async_remote_copy(
                src_ref=sens_out.at[peer],
                dst_ref=sens_in.at[me],
                send_sem=sens_ss.at[r],
                recv_sem=sens_rs.at[r],
                device_id={"trade": peer},
                device_id_type=MESH,
            ),
        )

    for r in range(1, nt):
        for copy in trade_copies(r):
            copy.start()
    sens_in[me] = sens_out[me]

    def send_state(r, c):
        pltpu.make_async_remote_copy(
            src_ref=st_out,
            dst_ref=st_in.at[mp],
            send_sem=st_ss,
            recv_sem=st_rs,
            device_id={"path": lax.rem(mp + r, npath)},
            device_id_type=MESH,
        ).start()
        return c

    lax.fori_loop(1, npath, send_state, 0)
    st_in[mp] = st_out[...]

    loads[5].wait()
    chi[...] = jnp.zeros_like(chi)
    clo[...] = jnp.zeros_like(clo)
    corr = corr_ref[...]
    top = corr.astype(BF)
    chi[0:nb, 0:nb] = top
    clo[0:nb, 0:nb] = (corr - top.astype(F32)).astype(BF)

    acc[...] = jnp.zeros_like(acc)
    hi_iota = lax.broadcasted_iota(jnp.int32, (HI, LANES), 0).astype(F32).astype(BF)
    lo_iota = lax.broadcasted_iota(jnp.int32, (LO, LANES), 0).astype(F32).astype(BF)
    one, zero = jnp.ones((), BF), jnp.zeros((), BF)

    def spread(ref, row, n):
        x = jnp.broadcast_to(ref[pl.ds(row, 1), :], (16, LANES)).astype(BF)
        return jnp.broadcast_to(x[None], (n // 16, 16, LANES)).reshape(n, LANES)

    def bucket_hot(row):
        return jnp.where(spread(lo_f, row, LO) == lo_iota, one, zero)

    def set_hot(row):
        return jnp.where(spread(hi_f, row, HI) == hi_iota, spread(s_f, row, HI), zero)

    def net_block(src):
        base = pl.multiple_of(src * rows, rows)
        cells = cell_in[src]
        h = lax.shift_right_logical(cells, 8)
        hi_f[pl.ds(base, rows), :] = h.astype(F32)
        lo_f[pl.ds(base, rows), :] = (cells - h * LO).astype(F32)
        s_f[pl.ds(base, rows), :] = sens_in[src].astype(F32)

        def step(g, c):
            row = base + g * 8
            left = jnp.concatenate([set_hot(row + i) for i in range(8)], axis=1)
            right = jnp.concatenate([bucket_hot(row + i) for i in range(8)], axis=1)
            acc[...] += lax.dot_general(left, right, NT, preferred_element_type=F32)
            return c

        lax.fori_loop(0, rows // 8, step, 0)

    net_block(me)

    def net_from(r, c):
        for copy in trade_copies(r):
            copy.wait_recv()
        net_block(lax.rem(me + nt - r, nt))
        return c

    lax.fori_loop(1, nt, net_from, 0)

    loads[6].wait()
    loads[7].wait()
    rw = jnp.concatenate([rw_ref[...].reshape(1, nb), jnp.zeros((1, GROUPS * LO - nb), F32)], axis=1)
    weighted = [acc[g * SETS : (g + 1) * SETS, :] * rw[:, g * LO : (g + 1) * LO] for g in range(GROUPS)]
    w = jnp.concatenate(weighted, axis=1)
    w_hi = w.astype(BF)
    w_lo = (w - w_hi.astype(F32)).astype(BF)
    cw = (
        jnp.dot(w_hi, chi[...], preferred_element_type=F32)
        + jnp.dot(w_hi, clo[...], preferred_element_type=F32)
        + jnp.dot(w_lo, chi[...], preferred_element_type=F32)
    )
    margin = jnp.sqrt(jnp.sum(w * cw, axis=1, keepdims=True) + 1.0)
    weight = dw_ref[me // (nt // DATES)]
    net_grad = ((weight * rw) * cw / margin).astype(BF)
    for g in range(GROUPS):
        grad[g * SETS : (g + 1) * SETS, :] = net_grad[:, g * LO : (g + 1) * LO]

    hi_iota8 = lax.broadcasted_iota(jnp.int32, (HI, LANES), 0).astype(F32)

    def pick_block(dst):
        base = pl.multiple_of(dst * rows, rows)

        def step(g, c):
            row = pl.multiple_of(base + g * 8, 8)
            right = jnp.concatenate([bucket_hot(row + i) for i in range(8)], axis=1)
            product = jnp.dot(grad[...], right, preferred_element_type=F32)
            for i in range(8):
                h = jnp.broadcast_to(hi_f[pl.ds(row + i, 1), :], (HI, LANES))
                kept = jnp.where(h == hi_iota8, product[:, i * LANES : (i + 1) * LANES], 0.0)
                tgp[i * 8 : (i + 1) * 8, :] = jnp.sum(kept.reshape(HI // 8, 8, LANES), axis=0)
            tot = tgp[pl.ds(0, 8, stride=8), :]
            for s in range(1, 8):
                tot = tot + tgp[pl.ds(s, 8, stride=8), :]
            tg[pl.ds(row, 8), :] = tot
            return c

        lax.fori_loop(0, rows // 8, step, 0)

    def pick_copy(r):
        peer = lax.rem(me + r, nt)
        return pltpu.make_async_remote_copy(
            src_ref=tg.at[pl.ds(pl.multiple_of(peer * rows, rows), rows)],
            dst_ref=tg_in.at[pl.ds(pl.multiple_of(me * rows, rows), rows)],
            send_sem=tg_ss.at[r],
            recv_sem=tg_rs.at[r],
            device_id={"trade": peer},
            device_id_type=MESH,
        )

    def pick_to(r, c):
        pick_block(lax.rem(me + r, nt))
        pick_copy(r).start()
        return c

    lax.fori_loop(1, nt, pick_to, 0)
    pick_block(me)
    own = pl.ds(pl.multiple_of(me * rows, rows), rows)
    tg_in[own, :] = tg[own, :]
    for r in range(1, nt):
        pick_copy(r).wait_recv()

    for c in range(rows):
        tgx[c] = tg_in[pl.ds(c, nt, stride=rows), :]

    def send_grad(r, c):
        peer = lax.rem(mp + r, npath)
        pltpu.make_async_remote_copy(
            src_ref=tgx.at[peer],
            dst_ref=pr.at[mp],
            send_sem=pr_ss,
            recv_sem=pr_rs,
            device_id={"path": peer},
            device_id_type=MESH,
        ).start()
        return c

    lax.fori_loop(1, npath, send_grad, 0)
    pr[mp] = tgx[mp]

    others = pl.ds(0, npath - 1)
    pltpu.make_async_copy(st_in.at[others], st_in.at[others], st_rs).wait()
    pairs = npath * nt
    ks = table_ref.shape[1]
    states = st_in[...].reshape(pairs, LANES)
    hot = (states == lax.broadcasted_iota(jnp.int32, (pairs, LANES), 1).astype(F32)).astype(F32).astype(BF)
    tab = table_ref[...].reshape(DATES * ks, LANES)
    at_date = lax.broadcasted_iota(jnp.int32, (DATES * ks, pairs), 0) // ks
    pair_date = (lax.broadcasted_iota(jnp.int32, (DATES * ks, pairs), 1) % nt) // (nt // DATES)
    basis = [
        jnp.where(
            at_date == pair_date, lax.dot_general(t, hot, NT, preferred_element_type=F32), 0.0
        ).astype(BF)
        for t in split3(tab)
    ]

    pltpu.make_async_copy(pr.at[others], pr.at[others], pr_rs).wait()
    right = pr[...].reshape(pairs, LANES).astype(BF)
    total = jnp.dot(basis[0], right, preferred_element_type=F32)
    for b in basis[1:]:
        total = total + jnp.dot(b, right, preferred_element_type=F32)
    out_ref[...] = total.reshape(DATES, ks, LANES)

    for r in range(1, nt):
        for copy in trade_copies(r):
            copy.wait_send()
        pick_copy(r).wait_send()
    pltpu.make_async_copy(st_in.at[others], st_in.at[others], st_ss).wait()
    pltpu.make_async_copy(pr.at[others], pr.at[others], pr_ss).wait()


def per_device(coef, set_ids, bucket_ids, states, table, risk_weight, correlation, date_weight):
    nt = lax.axis_size("trade")
    npath = lax.axis_size("path")
    trades = coef.shape[2]
    rows = trades // LANES
    nb = correlation.shape[0]
    ks = table.shape[1]
    vmem = pl.BlockSpec(memory_space=pltpu.VMEM)
    hbm = pl.BlockSpec(memory_space=pltpu.HBM)
    dma = pltpu.SemaphoreType.DMA
    return pl.pallas_call(
        functools.partial(kernel, nt, npath),
        out_shape=jax.ShapeDtypeStruct((DATES, ks, LANES), F32),
        in_specs=[hbm] * 8,
        out_specs=vmem,
        scratch_shapes=[
            pltpu.VMEM(coef.shape, F32),
            pltpu.VMEM((rows, LANES), jnp.int32),
            pltpu.VMEM((rows, LANES), jnp.int32),
            pltpu.SMEM(states.shape[::-1], jnp.int32),
            pltpu.VMEM(table.shape, F32),
            pltpu.VMEM((nb,), F32),
            pltpu.VMEM(correlation.shape, F32),
            pltpu.SMEM(date_weight.shape, F32),
            dma((8,)),
            pltpu.VMEM((rows * 8, LANES), F32),
            pltpu.VMEM((nt, rows, LANES), BF),
            pltpu.VMEM((nt, rows, LANES), BF),
            pltpu.VMEM((nt, rows, LANES), jnp.int32),
            pltpu.VMEM((nt * rows, LANES), F32),
            pltpu.VMEM((nt * rows, LANES), F32),
            pltpu.VMEM((nt * rows, LANES), F32),
            pltpu.VMEM((HI, LO), F32),
            pltpu.VMEM((GROUPS * LO, GROUPS * LO), BF),
            pltpu.VMEM((GROUPS * LO, GROUPS * LO), BF),
            pltpu.VMEM((HI, LO), BF),
            pltpu.VMEM((64, LANES), F32),
            pltpu.VMEM((nt * rows, LANES), F32),
            pltpu.VMEM((nt * rows, LANES), F32),
            pltpu.VMEM((npath, nt, LANES), F32),
            pltpu.VMEM((npath, nt, LANES), F32),
            pltpu.VMEM((nt, LANES), F32),
            pltpu.VMEM((npath, nt, LANES), F32),
            dma((nt,)),
            dma((nt,)),
            dma((nt,)),
            dma((nt,)),
            dma((nt,)),
            dma((nt,)),
            dma,
            dma,
            dma,
            dma,
        ],
        compiler_params=pltpu.CompilerParams(
            collective_id=0, has_side_effects=True, vmem_limit_bytes=62 * 1024 * 1024
        ),
    )(
        coef,
        set_ids.reshape(rows, LANES),
        bucket_ids.reshape(rows, LANES),
        states.T,
        table,
        risk_weight,
        correlation,
        date_weight,
    )


def solution(mesh):
    in_specs = (P(None, None, "trade"), P("trade"), P("trade"), P(None, "path"), P(), P(), P(), P())
    out_specs = P(None, None, ("trade", "path"))
    return jax.shard_map(
        per_device, mesh=mesh, in_specs=in_specs, out_specs=out_specs, check_vma=False
    )
```

```python
import functools

import jax
import jax.numpy as jnp
from jax import lax
from jax.experimental import pallas as pl
from jax.experimental.pallas import tpu as pltpu
from jax.sharding import PartitionSpec as P

DATES = 4
SETS = 64
LO = 256
GROUPS = 3
HI = GROUPS * SETS
LANES = 128
MESH = pl.DeviceIdType.MESH
BF = jnp.bfloat16
F32 = jnp.float32
NT = (((1,), (1,)), ((), ()))


def split3(x):
    a = x.astype(BF)
    r = x - a.astype(F32)
    b = r.astype(BF)
    c = (r - b.astype(F32)).astype(BF)
    return a, b, c


def kernel(
    nt,
    npath,
    coef_hbm,
    set_hbm,
    bkt_hbm,
    st_hbm,
    table_hbm,
    rw_hbm,
    corr_hbm,
    dw_hbm,
    out_ref,
    coef_ref,
    set_ref,
    bkt_ref,
    st_ref,
    table_ref,
    rw_ref,
    corr_ref,
    dw_ref,
    part,
    sens_out,
    sens_in,
    cell_in,
    hi_f,
    lo_f,
    s_f,
    acc,
    chi,
    clo,
    grad,
    tgp,
    tg,
    tg_in,
    tgx,
    msg,
    pr,
    st_out,
    st_in,
    load_sem,
    sens_ss,
    sens_rs,
    cell_ss,
    cell_rs,
    tg_ss,
    tg_rs,
    st_ss,
    st_rs,
    sib_ss,
    sib_rs,
    pr_ss,
    pr_rs,
):
    me = lax.axis_index("trade")
    mp = lax.axis_index("path")
    core = lax.rem(mp, 2)
    chip = mp // 2
    nchip = npath // 2
    rows = set_ref.shape[0]
    half = rows // 2
    nb = corr_ref.shape[0]
    per_date = nt // DATES

    def device(r, other):
        path = mp + other * (1 - 2 * core)
        return {"trade": lax.rem(me + r, nt), "path": path}

    def along(k):
        return {"path": lax.rem(chip + k, nchip) * 2 + core}

    loads = [
        pltpu.make_async_copy(src, dst, load_sem.at[i])
        for i, (src, dst) in enumerate(
            (
                (coef_hbm, coef_ref),
                (table_hbm, table_ref),
                (st_hbm, st_ref),
                (set_hbm, set_ref),
                (bkt_hbm, bkt_ref),
                (corr_hbm, corr_ref),
                (rw_hbm, rw_ref),
                (dw_hbm, dw_ref),
            )
        )
    ]
    for load in loads:
        load.start()

    barrier = pltpu.get_barrier_semaphore()
    for r in range(nt):
        for other in range(2):
            if r or other:
                pl.semaphore_signal(
                    barrier, inc=1, device_id=device(r, other), device_id_type=MESH
                )

    def greet(k, c):
        pl.semaphore_signal(barrier, inc=1, device_id=along(k), device_id_type=MESH)
        return c

    lax.fori_loop(1, nchip, greet, 0)

    loads[3].wait()
    loads[4].wait()
    for p in range(2):
        every = pl.ds(p, half, stride=2)
        bkt = bkt_ref[every, :]
        group = (bkt >= LO).astype(jnp.int32) + (bkt >= 2 * LO).astype(jnp.int32)
        cell_in[0, p * half : (p + 1) * half, :] = (
            (group * SETS + set_ref[every, :]) * LO + bkt - group * LO
        )

    for load in loads[:3]:
        load.wait()
    lane = lax.broadcasted_iota(jnp.int32, table_ref.shape[1:], 1)
    for d in range(DATES):
        for p in range(per_date):
            q = d * per_date + p
            state = st_ref[p, d]
            st_out[core, q : q + 1, :] = jnp.full((1, LANES), state, jnp.int32).astype(F32)
            col = jnp.sum(
                jnp.where(lane == state, table_ref[d], 0.0), axis=1, keepdims=True
            )
            for c in range(rows):
                x = coef_ref[d, :, c * LANES : (c + 1) * LANES] * col
                at = (c % 2) * half + c // 2
                part[at * 8 : (at + 1) * 8, :] = x[:8] + x[8:]
            tots = []
            for g in range(rows // 8):
                tot = part[pl.ds(g * 64, 8, stride=8), :]
                for s in range(1, 8):
                    tot = tot + part[pl.ds(g * 64 + s, 8, stride=8), :]
                tots.append(tot)
            sens_out[q] = jnp.concatenate(tots, axis=0).astype(BF)

    pl.semaphore_wait(barrier, 2 * nt - 1 + nchip - 1)

    def trade_copies(r):
        peer = lax.rem(me + r, nt)
        return (
            pltpu.make_async_remote_copy(
                src_ref=cell_in.at[0],
                dst_ref=cell_in.at[r],
                send_sem=cell_ss.at[r],
                recv_sem=cell_rs.at[r],
                device_id=device(r, 0),
                device_id_type=MESH,
            ),
            pltpu.make_async_remote_copy(
                src_ref=sens_out.at[peer],
                dst_ref=sens_in.at[r],
                send_sem=sens_ss.at[r],
                recv_sem=sens_rs.at[r],
                device_id=device(r, 0),
                device_id_type=MESH,
            ),
        )

    for r in range(1, nt):
        for copy in trade_copies(r):
            copy.start()
    sens_in[0] = sens_out[me]

    sibling = pltpu.make_async_remote_copy(
        src_ref=st_out.at[core],
        dst_ref=st_out.at[core],
        send_sem=sib_ss,
        recv_sem=sib_rs,
        device_id=device(0, 1),
        device_id_type=MESH,
    )
    sibling.start()

    loads[5].wait()
    chi[...] = jnp.zeros_like(chi)
    clo[...] = jnp.zeros_like(clo)
    corr = corr_ref[...]
    top = corr.astype(BF)
    chi[0:nb, 0:nb] = top
    clo[0:nb, 0:nb] = (corr - top.astype(F32)).astype(BF)

    hi_iota = lax.broadcasted_iota(jnp.int32, (HI, LANES), 0).astype(F32).astype(BF)
    lo_iota = lax.broadcasted_iota(jnp.int32, (LO, LANES), 0).astype(F32).astype(BF)
    lo_lane = lax.broadcasted_iota(jnp.int32, (LANES, LO), 1).astype(F32).astype(BF)
    one, zero = jnp.ones((), BF), jnp.zeros((), BF)

    def spread(ref, row, n):
        x = jnp.broadcast_to(ref[pl.ds(row, 1), :], (16, LANES)).astype(BF)
        return jnp.broadcast_to(x[None], (n // 16, 16, LANES)).reshape(n, LANES)

    def net_block(src):
        base = src * rows
        cells = cell_in[src]
        h = lax.shift_right_logical(cells, 8)
        low = (cells - h * LO).astype(F32)
        hi_f[base : base + rows, :] = h.astype(F32)
        lo_f[base : base + rows, :] = low
        s_f[base : base + rows, :] = sens_in[src].astype(F32)
        column = low.T.astype(BF)
        left, right = [], []
        for i in range(rows):
            left.append(
                jnp.where(
                    spread(hi_f, base + i, HI) == hi_iota, spread(s_f, base + i, HI), zero
                )
            )
            right.append(
                jnp.where(
                    jnp.broadcast_to(column[:, i : i + 1], (LANES, LO)) == lo_lane, one, zero
                )
            )
        return jnp.dot(
            jnp.concatenate(left, axis=1),
            jnp.concatenate(right, axis=0),
            preferred_element_type=F32,
        )

    acc[...] = net_block(0)

    for r in range(1, nt):
        for copy in trade_copies(r):
            copy.wait_recv()

    sibling.wait_recv()

    def state_copy(k):
        return pltpu.make_async_remote_copy(
            src_ref=st_out,
            dst_ref=st_in.at[chip],
            send_sem=st_ss,
            recv_sem=st_rs,
            device_id=along(k),
            device_id_type=MESH,
        )

    def send_state(k, c):
        state_copy(k).start()
        return c

    lax.fori_loop(1, nchip, send_state, 0)
    st_in[chip] = st_out[...]

    total = acc[...]
    for r in range(1, nt):
        total = total + net_block(r)
    acc[...] = total

    loads[6].wait()
    loads[7].wait()
    rw = jnp.concatenate(
        [rw_ref[...].reshape(1, nb), jnp.zeros((1, GROUPS * LO - nb), F32)], axis=1
    )
    weighted = [
        acc[g * SETS : (g + 1) * SETS, :] * rw[:, g * LO : (g + 1) * LO] for g in range(GROUPS)
    ]
    w = jnp.concatenate(weighted, axis=1)
    w_hi = w.astype(BF)
    w_lo = (w - w_hi.astype(F32)).astype(BF)
    cw = (
        jnp.dot(w_hi, chi[...], preferred_element_type=F32)
        + jnp.dot(w_hi, clo[...], preferred_element_type=F32)
        + jnp.dot(w_lo, chi[...], preferred_element_type=F32)
    )
    margin = jnp.sqrt(jnp.sum(w * cw, axis=1, keepdims=True) + 1.0)
    weight = dw_ref[me // per_date]
    net_grad = ((weight * rw) * cw / margin).astype(BF)
    for g in range(GROUPS):
        grad[g * SETS : (g + 1) * SETS, :] = net_grad[:, g * LO : (g + 1) * LO]

    def pick_block(dst, slot):
        base = pl.multiple_of(dst * rows, rows)
        right = jnp.concatenate(
            [
                jnp.where(spread(lo_f, base + i, LO) == lo_iota, one, zero)
                for i in range(rows)
            ],
            axis=1,
        )
        product = jnp.dot(grad[...], right, preferred_element_type=F32).astype(BF)
        for i in range(rows):
            kept = jnp.where(
                spread(hi_f, base + i, HI) == hi_iota,
                product[:, i * LANES : (i + 1) * LANES],
                zero,
            ).reshape(HI // 16, 16, LANES)
            tot = kept[0]
            for j in range(1, HI // 16):
                tot = tot + kept[j]
            tot = tot.astype(F32)
            tgp[slot, i * 8 : (i + 1) * 8, :] = tot[:8] + tot[8:]
        for p in range(2):
            tots = []
            for g in range(half // 8):
                at = (p * half + g * 8) * 8
                tot = tgp[slot, pl.ds(at, 8, stride=8), :]
                for s in range(1, 8):
                    tot = tot + tgp[slot, pl.ds(at + s, 8, stride=8), :]
                tots.append(tot)
            tg[dst, p] = jnp.concatenate(tots, axis=0).astype(BF)

    def pick_copy(r, other):
        return pltpu.make_async_remote_copy(
            src_ref=tg.at[lax.rem(nt - r, nt), core + other * (1 - 2 * core)],
            dst_ref=tg_in.at[core * nt + me],
            send_sem=tg_ss.at[2 * r + other],
            recv_sem=tg_rs.at[2 * r + other],
            device_id=device(r, other),
            device_id_type=MESH,
        )

    def pick_step(k, c):
        r = 2 * k + 1
        pick_block(nt - r, 0)
        pick_block(nt - r - 1, 1)
        pick_copy(r, 0).start()
        pick_copy(r, 1).start()
        pick_copy(lax.rem(r + 1, nt), 1).start()

        @pl.when(k < nt // 2 - 1)
        def _():
            pick_copy(r + 1, 0).start()

        return c

    lax.fori_loop(0, nt // 2, pick_step, 0)
    tg_in[core * nt + me] = tg[0, core]
    for r in range(nt):
        for other in range(2):
            if r or other:
                pick_copy(r, other).wait_recv()

    tgx[...] = tg_in[...].reshape(tgx.shape).astype(F32)
    for c in range(half):
        msg[c] = jnp.concatenate(
            [tgx[pl.ds(p * nt * half + c, nt, stride=half), :] for p in range(2)], axis=0
        ).astype(BF)

    def send_grad(k, c):
        pltpu.make_async_remote_copy(
            src_ref=msg.at[lax.rem(chip + k, nchip)],
            dst_ref=pr.at[chip],
            send_sem=pr_ss,
            recv_sem=pr_rs,
            device_id=along(k),
            device_id_type=MESH,
        ).start()
        return c

    lax.fori_loop(1, nchip, send_grad, 0)
    pr[chip] = msg[chip]

    others = pl.ds(0, nchip - 1)
    pltpu.make_async_copy(st_in.at[others], st_in.at[others], st_rs).wait()
    pairs = npath * nt
    ks = table_ref.shape[1]
    states = st_in[...].reshape(pairs, LANES)
    hot = jnp.where(
        states == lax.broadcasted_iota(jnp.int32, (pairs, LANES), 1).astype(F32), 1.0, 0.0
    ).astype(BF)
    tab = jnp.concatenate(split3(table_ref[...].reshape(DATES * ks, LANES)), axis=0)
    at_date = lax.rem(
        lax.broadcasted_iota(jnp.int32, (3 * DATES * ks, pairs), 0) // ks, DATES
    )
    pair_date = lax.rem(
        lax.broadcasted_iota(jnp.int32, (3 * DATES * ks, pairs), 1), nt
    ) // per_date
    basis = jnp.where(
        at_date == pair_date, lax.dot_general(tab, hot, NT, preferred_element_type=F32), 0.0
    ).astype(BF)

    pltpu.make_async_copy(pr.at[others], pr.at[others], pr_rs).wait()
    total = jnp.dot(basis, pr[...].reshape(pairs, LANES), preferred_element_type=F32)
    total = total.reshape(3, DATES, ks, LANES)
    out_ref[...] = total[0] + total[1] + total[2]

    for r in range(1, nt):
        for copy in trade_copies(r):
            copy.wait_send()
    for r in range(nt):
        for other in range(2):
            if r or other:
                pick_copy(r, other).wait_send()
    sibling.wait_send()
    pltpu.make_async_copy(st_in.at[others], st_in.at[others], st_ss).wait()
    pltpu.make_async_copy(pr.at[others], pr.at[others], pr_ss).wait()


def per_device(coef, set_ids, bucket_ids, states, table, risk_weight, correlation, date_weight):
    nt = lax.axis_size("trade")
    npath = lax.axis_size("path")
    trades = coef.shape[2]
    rows = trades // LANES
    nb = correlation.shape[0]
    ks = table.shape[1]
    vmem = pl.BlockSpec(memory_space=pltpu.VMEM)
    hbm = pl.BlockSpec(memory_space=pltpu.HBM)
    dma = pltpu.SemaphoreType.DMA
    return pl.pallas_call(
        functools.partial(kernel, nt, npath),
        out_shape=jax.ShapeDtypeStruct((DATES, ks, LANES), F32),
        in_specs=[hbm] * 8,
        out_specs=vmem,
        scratch_shapes=[
            pltpu.VMEM(coef.shape, F32),
            pltpu.VMEM((rows, LANES), jnp.int32),
            pltpu.VMEM((rows, LANES), jnp.int32),
            pltpu.SMEM(states.shape[::-1], jnp.int32),
            pltpu.VMEM(table.shape, F32),
            pltpu.VMEM((nb,), F32),
            pltpu.VMEM(correlation.shape, F32),
            pltpu.SMEM(date_weight.shape, F32),
            pltpu.VMEM((rows * 8, LANES), F32),
            pltpu.VMEM((nt, rows, LANES), BF),
            pltpu.VMEM((nt, rows, LANES), BF),
            pltpu.VMEM((nt, rows, LANES), jnp.int32),
            pltpu.VMEM((nt * rows, LANES), F32),
            pltpu.VMEM((nt * rows, LANES), F32),
            pltpu.VMEM((nt * rows, LANES), F32),
            pltpu.VMEM((HI, LO), F32),
            pltpu.VMEM((GROUPS * LO, GROUPS * LO), BF),
            pltpu.VMEM((GROUPS * LO, GROUPS * LO), BF),
            pltpu.VMEM((HI, LO), BF),
            pltpu.VMEM((2, rows * 8, LANES), F32),
            pltpu.VMEM((nt, 2, rows // 2, LANES), BF),
            pltpu.VMEM((2 * nt, rows // 2, LANES), BF),
            pltpu.VMEM((nt * rows, LANES), F32),
            pltpu.VMEM((npath // 2, 2 * nt, LANES), BF),
            pltpu.VMEM((npath // 2, 2 * nt, LANES), BF),
            pltpu.VMEM((2, nt, LANES), F32),
            pltpu.VMEM((npath // 2, 2, nt, LANES), F32),
            dma((8,)),
            dma((nt,)),
            dma((nt,)),
            dma((nt,)),
            dma((nt,)),
            dma((2 * nt,)),
            dma((2 * nt,)),
            dma,
            dma,
            dma,
            dma,
            dma,
            dma,
        ],
        compiler_params=pltpu.CompilerParams(
            collective_id=0, has_side_effects=True, vmem_limit_bytes=62 * 1024 * 1024
        ),
    )(
        coef,
        set_ids.reshape(rows, LANES),
        bucket_ids.reshape(rows, LANES),
        states.T,
        table,
        risk_weight,
        correlation,
        date_weight,
    )


def solution(mesh):
    in_specs = (P(None, None, "trade"), P("trade"), P("trade"), P(None, "path"), P(), P(), P(), P())
    out_specs = P(None, None, ("trade", "path"))
    return jax.shard_map(
        per_device, mesh=mesh, in_specs=in_specs, out_specs=out_specs, check_vma=False
    )
```

```python
import functools

import jax
import jax.numpy as jnp
from jax import lax
from jax.experimental import pallas as pl
from jax.experimental.pallas import tpu as pltpu
from jax.sharding import PartitionSpec as P

DATES = 4
SETS = 64
LO = 256
GROUPS = 3
HI = GROUPS * SETS
LANES = 128
MESH = pl.DeviceIdType.MESH
BF = jnp.bfloat16
F32 = jnp.float32
NT = (((1,), (1,)), ((), ()))


def split3(x):
    a = x.astype(BF)
    r = x - a.astype(F32)
    b = r.astype(BF)
    c = (r - b.astype(F32)).astype(BF)
    return a, b, c


def kernel(
    nt,
    npath,
    coef_hbm,
    set_hbm,
    bkt_hbm,
    st_hbm,
    table_hbm,
    rw_hbm,
    corr_hbm,
    dw_hbm,
    out_ref,
    coef_ref,
    set_ref,
    bkt_ref,
    st_ref,
    table_ref,
    rw_ref,
    corr_ref,
    dw_ref,
    part,
    sens_out,
    sens_in,
    cell_in,
    hi_f,
    lo_f,
    s_f,
    acc,
    chi,
    clo,
    grad,
    tgp,
    tg,
    tg_in,
    msg,
    pr,
    st_out,
    st_in,
    load_sem,
    sens_ss,
    sens_rs,
    cell_ss,
    cell_rs,
    tg_ss,
    tg_rs,
    st_ss,
    st_rs,
    sib_ss,
    sib_rs,
    pr_ss,
    pr_rs,
):
    me = lax.axis_index("trade")
    mp = lax.axis_index("path")
    core = lax.rem(mp, 2)
    chip = mp // 2
    nchip = npath // 2
    rows = set_ref.shape[0]
    half = rows // 2
    nb = corr_ref.shape[0]
    per_date = nt // DATES
    ring = nchip // 2
    quarter = ring // 2

    def device(r, other):
        path = mp + other * (1 - 2 * core)
        return {"trade": lax.rem(me + r, nt), "path": path}

    def along(k):
        return {"path": lax.rem(chip + k, nchip) * 2 + core}

    loads = [
        pltpu.make_async_copy(src, dst, load_sem.at[i])
        for i, (src, dst) in enumerate(
            [
                (set_hbm, set_ref),
                (bkt_hbm, bkt_ref),
                (st_hbm, st_ref),
                (table_hbm, table_ref),
            ]
            + [(coef_hbm.at[d], coef_ref.at[d]) for d in range(DATES)]
            + [
                (corr_hbm, corr_ref),
                (rw_hbm, rw_ref),
                (dw_hbm, dw_ref),
            ]
        )
    ]
    for load in loads:
        load.start()

    barrier = pltpu.get_barrier_semaphore()
    for r in range(nt):
        for other in range(2):
            if r or other:
                pl.semaphore_signal(
                    barrier, inc=1, device_id=device(r, other), device_id_type=MESH
                )

    def greet(k, c):
        pl.semaphore_signal(barrier, inc=1, device_id=along(k), device_id_type=MESH)
        return c

    lax.fori_loop(1, nchip, greet, 0)

    def place(c):
        y, z, k = c // (2 * ring), c // 2 % ring, c % 2
        return ((z // quarter * 2 + k) * 2 + y) * quarter + z % quarter

    loads[0].wait()
    loads[1].wait()
    for c in range(rows):
        if c // 2 % quarter == 0:
            every = pl.ds(c, quarter, stride=2)
            bkt = bkt_ref[every, :]
            group = (bkt >= LO).astype(jnp.int32) + (bkt >= 2 * LO).astype(jnp.int32)
            cell_in[0, place(c) : place(c) + quarter, :] = (
                (group * SETS + set_ref[every, :]) * LO + bkt - group * LO
            )

    def trade_copies(r):
        return (
            pltpu.make_async_remote_copy(
                src_ref=cell_in.at[0],
                dst_ref=cell_in.at[r],
                send_sem=cell_ss.at[r],
                recv_sem=cell_rs.at[r],
                device_id=device(r, 0),
                device_id_type=MESH,
            ),
            pltpu.make_async_remote_copy(
                src_ref=sens_out.at[r],
                dst_ref=sens_in.at[r],
                send_sem=sens_ss.at[r],
                recv_sem=sens_rs.at[r],
                device_id=device(r, 0),
                device_id_type=MESH,
            ),
        )

    pl.semaphore_wait(barrier, 2 * nt - 1 + nchip - 1)
    far = sorted(range(nt), key=lambda r: -min(r, nt - r))
    for r in far[:-1]:
        trade_copies(r)[0].start()

    for load in loads[2 : 4 + DATES]:
        load.wait()
    lane = lax.broadcasted_iota(jnp.int32, table_ref.shape[1:], 1)
    for r in far:
        q = lax.rem(me + r, nt)
        d = q // per_date
        state = st_ref[lax.rem(q, per_date), d]
        col = jnp.sum(jnp.where(lane == state, table_ref[d], 0.0), axis=1, keepdims=True)
        for c in range(rows):
            x = coef_ref[d, :, c * LANES : (c + 1) * LANES] * col
            at = place(c)
            part[at * 8 : (at + 1) * 8, :] = x[:8] + x[8:]
        tots = []
        for g in range(rows // 8):
            tot = part[pl.ds(g * 64, 8, stride=8), :]
            for s in range(1, 8):
                tot = tot + part[pl.ds(g * 64 + s, 8, stride=8), :]
            tots.append(tot)
        if r:
            sens_out[r] = jnp.concatenate(tots, axis=0).astype(BF)
            trade_copies(r)[1].start()
        else:
            sens_in[0] = jnp.concatenate(tots, axis=0).astype(BF)

    for d in range(DATES):
        for p in range(per_date):
            q = d * per_date + p
            st_out[q : q + 1, :] = jnp.full((1, LANES), st_ref[p, d], jnp.int32).astype(F32)

    def send_state(k, c):
        pltpu.make_async_remote_copy(
            src_ref=st_out,
            dst_ref=st_in.at[core, chip],
            send_sem=st_ss,
            recv_sem=st_rs,
            device_id=along(k),
            device_id_type=MESH,
        ).start()
        return c

    lax.fori_loop(1, nchip, send_state, 0)
    st_in[core, chip] = st_out[...]
    others = pl.ds(0, nchip - 1)
    sibling = pltpu.make_async_remote_copy(
        src_ref=st_in.at[core],
        dst_ref=st_in.at[core],
        send_sem=sib_ss,
        recv_sem=sib_rs,
        device_id=device(0, 1),
        device_id_type=MESH,
    )

    loads[4 + DATES].wait()
    chi[...] = jnp.zeros_like(chi)
    clo[...] = jnp.zeros_like(clo)
    corr = corr_ref[...]
    top = corr.astype(BF)
    chi[0:nb, 0:nb] = top
    clo[0:nb, 0:nb] = (corr - top.astype(F32)).astype(BF)

    hi_iota = lax.broadcasted_iota(jnp.int32, (HI, LANES), 0).astype(F32).astype(BF)
    lo_iota = lax.broadcasted_iota(jnp.int32, (LO, LANES), 0).astype(F32).astype(BF)
    lo_lane = lax.broadcasted_iota(jnp.int32, (LANES, LO), 1).astype(F32).astype(BF)
    one, zero = jnp.ones((), BF), jnp.zeros((), BF)

    def spread(ref, row, n):
        x = jnp.broadcast_to(ref[pl.ds(row, 1), :], (16, LANES)).astype(BF)
        return jnp.broadcast_to(x[None], (n // 16, 16, LANES)).reshape(n, LANES)

    def net_block(src):
        base = src * rows
        cells = cell_in[src]
        h = lax.shift_right_logical(cells, 8)
        low = (cells - h * LO).astype(F32)
        hi_f[base : base + rows, :] = h.astype(F32)
        lo_f[base : base + rows, :] = low
        s_f[base : base + rows, :] = sens_in[src].astype(F32)
        column = low.T.astype(BF)
        left, right = [], []
        for i in range(rows):
            left.append(
                jnp.where(
                    spread(hi_f, base + i, HI) == hi_iota, spread(s_f, base + i, HI), zero
                )
            )
            right.append(
                jnp.where(
                    jnp.broadcast_to(column[:, i : i + 1], (LANES, LO)) == lo_lane, one, zero
                )
            )
        return jnp.dot(
            jnp.concatenate(left, axis=1),
            jnp.concatenate(right, axis=0),
            preferred_element_type=F32,
        )

    acc[...] = net_block(0)

    for r in range(1, nt):
        for copy in trade_copies(r):
            copy.wait_recv()

    total = acc[...]
    for r in range(1, nt):
        total = total + net_block(r)
    acc[...] = total

    pltpu.make_async_copy(st_in.at[core, others], st_in.at[core, others], st_rs).wait()
    sibling.start()

    loads[5 + DATES].wait()
    loads[6 + DATES].wait()
    rw = jnp.concatenate(
        [rw_ref[...].reshape(1, nb), jnp.zeros((1, GROUPS * LO - nb), F32)], axis=1
    )
    weighted = [
        acc[g * SETS : (g + 1) * SETS, :] * rw[:, g * LO : (g + 1) * LO] for g in range(GROUPS)
    ]
    w = jnp.concatenate(weighted, axis=1)
    w_hi = w.astype(BF)
    w_lo = (w - w_hi.astype(F32)).astype(BF)
    cw = (
        jnp.dot(w_hi, chi[...], preferred_element_type=F32)
        + jnp.dot(w_hi, clo[...], preferred_element_type=F32)
        + jnp.dot(w_lo, chi[...], preferred_element_type=F32)
    )
    margin = jnp.sqrt(jnp.sum(w * cw, axis=1, keepdims=True) + 1.0)
    weight = dw_ref[me // per_date]
    net_grad = ((weight * rw) * cw / margin).astype(BF)
    for g in range(GROUPS):
        grad[g * SETS : (g + 1) * SETS, :] = net_grad[:, g * LO : (g + 1) * LO]

    def pick_blocks(dst, h, slot):
        def row(i):
            return pl.multiple_of(dst * rows + h * half, half) + i // half * rows + i % half

        right = jnp.concatenate(
            [
                jnp.where(spread(lo_f, row(i), LO) == lo_iota, one, zero)
                for i in range(rows)
            ],
            axis=1,
        )
        product = jnp.dot(grad[...], right, preferred_element_type=F32).astype(BF)
        for i in range(rows):
            kept = jnp.where(
                spread(hi_f, row(i), HI) == hi_iota,
                product[:, i * LANES : (i + 1) * LANES],
                zero,
            ).reshape(HI // 16, 16, LANES)
            tot = kept[0]
            for j in range(1, HI // 16):
                tot = tot + kept[j]
            tot = tot.astype(F32)
            tgp[slot, i * 8 : (i + 1) * 8, :] = tot[:8] + tot[8:]
        for b in range(2):
            for k in range(2):
                at = (b * half + k * 8) * 8
                tot = tgp[slot, pl.ds(at, 8, stride=8), :]
                for s in range(1, 8):
                    tot = tot + tgp[slot, pl.ds(at + s, 8, stride=8), :]
                tg[dst + b, h, k] = tot

    def pick_copy(r, h, other):
        return pltpu.make_async_remote_copy(
            src_ref=tg.at[lax.rem(nt - r, nt), h, core + other * (1 - 2 * core)],
            dst_ref=tg_in.at[h, pl.ds(pl.multiple_of((core * nt + me) * 8, 8), 8)],
            send_sem=tg_ss.at[(h * nt + r) * 2 + other],
            recv_sem=tg_rs.at[(h * nt + r) * 2 + other],
            device_id=device(r, other),
            device_id_type=MESH,
        )

    def pick_step(n, c):
        h = n // 2
        first = (1 - lax.rem(n, 2)) * (nt // 2)
        pick_blocks(first + 2, h, 0)
        pick_blocks(first, h, 1)
        for b in range(nt // 2 - 1, 0, -1):
            for other in range(2):
                pick_copy(nt - first - b, h, other).start()
        pick_copy(lax.rem(nt - first, nt), h, 1).start()

        @pl.when(first > 0)
        def _():
            pick_copy(lax.rem(nt - first, nt), h, 0).start()

        return c

    lax.fori_loop(0, 4, pick_step, 0)

    mine = pl.ds(pl.multiple_of((core * nt + me) * 8, 8), 8)
    for h in range(2):
        tg_in[h, mine, :] = tg[0, h, core]

    def send_grad(target):
        return pltpu.make_async_remote_copy(
            src_ref=msg.at[target],
            dst_ref=pr.at[chip],
            send_sem=pr_ss,
            recv_sem=pr_rs,
            device_id={"path": target * 2 + core},
            device_id_type=MESH,
        )

    y, z = chip // ring, lax.rem(chip, ring)
    for h in range(2):
        for r in range(nt):
            for other in range(2):
                if r or other:
                    pick_copy(r, h, other).wait_recv()
        for c in range(half // 2):
            msg[c // quarter * ring + h * quarter + c % quarter] = jnp.concatenate(
                [tg_in[h, pl.ds(k * nt * 8 + c, nt, stride=8), :] for k in range(2)], axis=0
            ).astype(BF)
        for k in range(half // 2 - 1, 0, -1):
            to_z = h * quarter + lax.rem(z + k, quarter)
            send_grad(lax.rem(y + k // quarter, 2) * ring + to_z).start()
        same = y * ring + h * quarter + lax.rem(z, quarter)

        @pl.when(same != chip)
        def _():
            send_grad(same).start()

    pr[chip] = msg[chip]

    sibling.wait_recv()
    pairs = npath * nt
    ks = table_ref.shape[1]
    states = jnp.concatenate([st_in[k, c] for c in range(nchip) for k in range(2)], axis=0)
    hot = jnp.where(
        states == lax.broadcasted_iota(jnp.int32, (pairs, LANES), 1).astype(F32), 1.0, 0.0
    ).astype(BF)
    tab = jnp.concatenate(split3(table_ref[...].reshape(DATES * ks, LANES)), axis=0)
    at_date = lax.rem(
        lax.broadcasted_iota(jnp.int32, (3 * DATES * ks, pairs), 0) // ks, DATES
    )
    pair_date = lax.rem(
        lax.broadcasted_iota(jnp.int32, (3 * DATES * ks, pairs), 1), nt
    ) // per_date
    basis = jnp.where(
        at_date == pair_date, lax.dot_general(tab, hot, NT, preferred_element_type=F32), 0.0
    ).astype(BF)

    pltpu.make_async_copy(pr.at[others], pr.at[others], pr_rs).wait()
    total = jnp.dot(basis, pr[...].reshape(pairs, LANES), preferred_element_type=F32)
    total = total.reshape(3, DATES, ks, LANES)
    out_ref[...] = total[0] + total[1] + total[2]

    for r in range(1, nt):
        for copy in trade_copies(r):
            copy.wait_send()
    for r in range(nt):
        for other in range(2):
            if r or other:
                pick_copy(r, 0, other).wait_send()
                pick_copy(r, 1, other).wait_send()
    sibling.wait_send()
    pltpu.make_async_copy(st_in.at[core, others], st_in.at[core, others], st_ss).wait()
    pltpu.make_async_copy(pr.at[others], pr.at[others], pr_ss).wait()


def per_device(coef, set_ids, bucket_ids, states, table, risk_weight, correlation, date_weight):
    nt = lax.axis_size("trade")
    npath = lax.axis_size("path")
    trades = coef.shape[2]
    rows = trades // LANES
    nb = correlation.shape[0]
    ks = table.shape[1]
    vmem = pl.BlockSpec(memory_space=pltpu.VMEM)
    hbm = pl.BlockSpec(memory_space=pltpu.HBM)
    dma = pltpu.SemaphoreType.DMA
    return pl.pallas_call(
        functools.partial(kernel, nt, npath),
        out_shape=jax.ShapeDtypeStruct((DATES, ks, LANES), F32),
        in_specs=[hbm] * 8,
        out_specs=vmem,
        scratch_shapes=[
            pltpu.VMEM(coef.shape, F32),
            pltpu.VMEM((rows, LANES), jnp.int32),
            pltpu.VMEM((rows, LANES), jnp.int32),
            pltpu.SMEM(states.shape[::-1], jnp.int32),
            pltpu.VMEM(table.shape, F32),
            pltpu.VMEM((nb,), F32),
            pltpu.VMEM(correlation.shape, F32),
            pltpu.SMEM(date_weight.shape, F32),
            pltpu.VMEM((rows * 8, LANES), F32),
            pltpu.VMEM((nt, rows, LANES), BF),
            pltpu.VMEM((nt, rows, LANES), BF),
            pltpu.VMEM((nt, rows, LANES), jnp.int32),
            pltpu.VMEM((nt * rows, LANES), F32),
            pltpu.VMEM((nt * rows, LANES), F32),
            pltpu.VMEM((nt * rows, LANES), F32),
            pltpu.VMEM((HI, LO), F32),
            pltpu.VMEM((GROUPS * LO, GROUPS * LO), BF),
            pltpu.VMEM((GROUPS * LO, GROUPS * LO), BF),
            pltpu.VMEM((HI, LO), BF),
            pltpu.VMEM((2, rows * 8, LANES), F32),
            pltpu.VMEM((nt, 2, 2, 8, LANES), F32),
            pltpu.VMEM((2, 2 * nt * 8, LANES), F32),
            pltpu.VMEM((npath // 2, 2 * nt, LANES), BF),
            pltpu.VMEM((npath // 2, 2 * nt, LANES), BF),
            pltpu.VMEM((nt, LANES), F32),
            pltpu.VMEM((2, npath // 2, nt, LANES), F32),
            dma((7 + DATES,)),
            dma((nt,)),
            dma((nt,)),
            dma((nt,)),
            dma((nt,)),
            dma((4 * nt,)),
            dma((4 * nt,)),
            dma,
            dma,
            dma,
            dma,
            dma,
            dma,
        ],
        compiler_params=pltpu.CompilerParams(
            collective_id=0, has_side_effects=True, vmem_limit_bytes=62 * 1024 * 1024
        ),
    )(
        coef,
        set_ids.reshape(rows, LANES),
        bucket_ids.reshape(rows, LANES),
        states.T,
        table,
        risk_weight,
        correlation,
        date_weight,
    )


def solution(mesh):
    in_specs = (P(None, None, "trade"), P("trade"), P("trade"), P(None, "path"), P(), P(), P(), P())
    out_specs = P(None, None, ("trade", "path"))
    return jax.shard_map(
        per_device, mesh=mesh, in_specs=in_specs, out_specs=out_specs, check_vma=False
    )
```

```python
import functools

import jax
import jax.numpy as jnp
from jax import lax
from jax.experimental import pallas as pl
from jax.experimental.pallas import tpu as pltpu
from jax.sharding import PartitionSpec as P

DATES = 4
SETS = 64
LO = 256
GROUPS = 3
HI = GROUPS * SETS
LANES = 128
MESH = pl.DeviceIdType.MESH
BF = jnp.bfloat16
F32 = jnp.float32
NT = (((1,), (1,)), ((), ()))


def split3(x):
    a = x.astype(BF)
    r = x - a.astype(F32)
    b = r.astype(BF)
    c = (r - b.astype(F32)).astype(BF)
    return a, b, c


def kernel(
    nt,
    npath,
    coef_hbm,
    set_hbm,
    bkt_hbm,
    st_hbm,
    table_hbm,
    rw_hbm,
    corr_hbm,
    dw_hbm,
    out_ref,
    coef_ref,
    set_ref,
    bkt_ref,
    st_ref,
    table_ref,
    rw_ref,
    corr_ref,
    dw_ref,
    part,
    sens_out,
    sens_in,
    cell_in,
    hi_f,
    lo_f,
    s_f,
    acc,
    chi,
    clo,
    grad,
    tgp,
    tg,
    tg_in,
    msg,
    pr,
    st_out,
    st_in,
    load_sem,
    sens_ss,
    sens_rs,
    cell_ss,
    cell_rs,
    tg_ss,
    tg_rs,
    st_ss,
    st_rs,
    sib_ss,
    sib_rs,
    pr_ss,
    pr_rs,
):
    me = lax.axis_index("trade")
    mp = lax.axis_index("path")
    core = lax.rem(mp, 2)
    chip = mp // 2
    nchip = npath // 2
    rows = set_ref.shape[0]
    half = rows // 2
    nb = corr_ref.shape[0]
    wide = chi.shape[0]
    per_date = nt // DATES
    ring = nchip // 2
    quarter = ring // 2

    def device(r, other):
        path = mp + other * (1 - 2 * core)
        return {"trade": lax.rem(me + r, nt), "path": path}

    def along(k):
        return {"path": lax.rem(chip + k, nchip) * 2 + core}

    loads = [
        pltpu.make_async_copy(src, dst, load_sem.at[i])
        for i, (src, dst) in enumerate(
            [
                (set_hbm, set_ref),
                (bkt_hbm, bkt_ref),
                (st_hbm, st_ref),
                (table_hbm, table_ref),
            ]
            + [(coef_hbm.at[d], coef_ref.at[d]) for d in range(DATES)]
            + [
                (corr_hbm, corr_ref),
                (rw_hbm, rw_ref),
                (dw_hbm, dw_ref),
            ]
        )
    ]
    for load in loads:
        load.start()

    barrier = pltpu.get_barrier_semaphore()
    for r in range(nt):
        for other in range(2):
            if r or other:
                pl.semaphore_signal(
                    barrier, inc=1, device_id=device(r, other), device_id_type=MESH
                )

    def greet(k, c):
        pl.semaphore_signal(barrier, inc=1, device_id=along(k), device_id_type=MESH)
        return c

    lax.fori_loop(1, nchip, greet, 0)

    def place(c):
        y, z, k = c // (2 * ring), c // 2 % ring, c % 2
        return ((z // quarter * 2 + k) * 2 + y) * quarter + z % quarter

    loads[0].wait()
    loads[1].wait()
    for c in range(rows):
        if c // 2 % quarter == 0:
            every = pl.ds(c, quarter, stride=2)
            bkt = bkt_ref[every, :]
            group = (bkt >= LO).astype(jnp.int32) + (bkt >= 2 * LO).astype(jnp.int32)
            cell_in[0, place(c) : place(c) + quarter, :] = (
                (group * SETS + set_ref[every, :]) * LO + bkt - group * LO
            )

    def trade_copies(r):
        return (
            pltpu.make_async_remote_copy(
                src_ref=cell_in.at[0],
                dst_ref=cell_in.at[r],
                send_sem=cell_ss.at[r],
                recv_sem=cell_rs.at[r],
                device_id=device(r, 0),
                device_id_type=MESH,
            ),
            pltpu.make_async_remote_copy(
                src_ref=sens_out.at[r],
                dst_ref=sens_in.at[r],
                send_sem=sens_ss.at[r],
                recv_sem=sens_rs.at[r],
                device_id=device(r, 0),
                device_id_type=MESH,
            ),
        )

    far = sorted(range(nt), key=lambda r: -min(r, nt - r))

    for load in loads[2 : 4 + DATES]:
        load.wait()
    lane = lax.broadcasted_iota(jnp.int32, table_ref.shape[1:], 1)
    for r in far:
        q = lax.rem(me + r, nt)
        d = q // per_date
        state = st_ref[lax.rem(q, per_date), d]
        col = jnp.sum(jnp.where(lane == state, table_ref[d], 0.0), axis=1, keepdims=True)
        for c in range(rows):
            x = coef_ref[d, :, c * LANES : (c + 1) * LANES] * col
            at = place(c)
            part[at * 8 : (at + 1) * 8, :] = x[:8] + x[8:]
        tots = []
        for g in range(rows // 8):
            tot = part[pl.ds(g * 64, 8, stride=8), :]
            for s in range(1, 8):
                tot = tot + part[pl.ds(g * 64 + s, 8, stride=8), :]
            tots.append(tot)
        if r:
            sens_out[r] = jnp.concatenate(tots, axis=0).astype(BF)
        else:
            sens_in[0] = jnp.concatenate(tots, axis=0).astype(BF)

    pl.semaphore_wait(barrier, 2 * nt - 1 + nchip - 1)
    for r in far[:-1]:
        for copy in trade_copies(r):
            copy.start()

    for d in range(DATES):
        for p in range(per_date):
            q = d * per_date + p
            st_out[q : q + 1, :] = jnp.full((1, LANES), st_ref[p, d], jnp.int32).astype(F32)

    def send_state(k, c):
        pltpu.make_async_remote_copy(
            src_ref=st_out,
            dst_ref=st_in.at[core, chip],
            send_sem=st_ss,
            recv_sem=st_rs,
            device_id=along(k),
            device_id_type=MESH,
        ).start()
        return c

    lax.fori_loop(1, nchip, send_state, 0)
    st_in[core, chip] = st_out[...]
    others = pl.ds(0, nchip - 1)
    sibling = pltpu.make_async_remote_copy(
        src_ref=st_in.at[core],
        dst_ref=st_in.at[core],
        send_sem=sib_ss,
        recv_sem=sib_rs,
        device_id=device(0, 1),
        device_id_type=MESH,
    )

    loads[4 + DATES].wait()
    chi[...] = jnp.zeros_like(chi)
    clo[...] = jnp.zeros_like(clo)
    corr = corr_ref[...]
    top = corr.astype(BF)
    chi[0:nb, 0:nb] = top
    clo[0:nb, 0:nb] = (corr - top.astype(F32)).astype(BF)

    hi_iota = lax.broadcasted_iota(jnp.int32, (HI, LANES), 0).astype(F32).astype(BF)
    lo_iota = lax.broadcasted_iota(jnp.int32, (LO, LANES), 0).astype(F32).astype(BF)
    lo_lane = lax.broadcasted_iota(jnp.int32, (LANES, LO), 1).astype(F32).astype(BF)
    one, zero = jnp.ones((), BF), jnp.zeros((), BF)

    def spread(ref, row, n):
        x = jnp.broadcast_to(ref[pl.ds(row, 1), :], (16, LANES)).astype(BF)
        return jnp.broadcast_to(x[None], (n // 16, 16, LANES)).reshape(n, LANES)

    def net_block(src):
        base = src * rows
        cells = cell_in[src]
        h = lax.shift_right_logical(cells, 8)
        low = (cells - h * LO).astype(F32)
        hi_f[base : base + rows, :] = h.astype(F32)
        lo_f[base : base + rows, :] = low
        s_f[base : base + rows, :] = sens_in[src].astype(F32)
        column = low.T.astype(BF)
        left, right = [], []
        for i in range(rows):
            left.append(
                jnp.where(
                    spread(hi_f, base + i, HI) == hi_iota, spread(s_f, base + i, HI), zero
                )
            )
            right.append(
                jnp.where(
                    jnp.broadcast_to(column[:, i : i + 1], (LANES, LO)) == lo_lane, one, zero
                )
            )
        return jnp.dot(
            jnp.concatenate(left, axis=1),
            jnp.concatenate(right, axis=0),
            preferred_element_type=F32,
        )

    acc[...] = net_block(0)

    for r in range(1, nt):
        for copy in trade_copies(r):
            copy.wait_recv()

    total = acc[...]
    for r in range(1, nt):
        total = total + net_block(r)
    acc[...] = total

    pltpu.make_async_copy(st_in.at[core, others], st_in.at[core, others], st_rs).wait()
    sibling.start()

    loads[5 + DATES].wait()
    loads[6 + DATES].wait()
    rw = jnp.concatenate(
        [rw_ref[...].reshape(1, nb), jnp.zeros((1, wide - nb), F32)], axis=1
    )
    netted = jnp.concatenate(
        [
            acc[g * SETS : (g + 1) * SETS, : min(LO, wide - g * LO)]
            for g in range(GROUPS)
        ],
        axis=1,
    )
    w = netted * rw
    w_hi = w.astype(BF)
    w_lo = (w - w_hi.astype(F32)).astype(BF)
    both = jnp.dot(
        jnp.concatenate([w_hi, w_lo], axis=0), chi[...], preferred_element_type=F32
    )
    cw = both[:SETS] + both[SETS:] + jnp.dot(w_hi, clo[...], preferred_element_type=F32)
    margin = jnp.sqrt(jnp.sum(w * cw, axis=1, keepdims=True) + 1.0)
    weight = dw_ref[me // per_date]
    net_grad = ((weight * rw) * cw / margin).astype(BF)
    for g in range(GROUPS):
        part_g = net_grad[:, g * LO : min((g + 1) * LO, wide)]
        grad[g * SETS : (g + 1) * SETS, : part_g.shape[1]] = part_g
    grad[(GROUPS - 1) * SETS :, wide - (GROUPS - 1) * LO :] = jnp.zeros(
        (SETS, GROUPS * LO - wide), BF
    )

    def pick_blocks(dst, h, slot):
        def row(i):
            return pl.multiple_of(dst * rows + h * half, half) + i // half * rows + i % half

        right = jnp.concatenate(
            [
                jnp.where(spread(lo_f, row(i), LO) == lo_iota, one, zero)
                for i in range(rows)
            ],
            axis=1,
        )
        product = jnp.dot(grad[...], right, preferred_element_type=F32).astype(BF)
        for i in range(rows):
            kept = jnp.where(
                spread(hi_f, row(i), HI) == hi_iota,
                product[:, i * LANES : (i + 1) * LANES],
                zero,
            ).reshape(HI // 16, 16, LANES)
            tot = kept[0]
            for j in range(1, HI // 16):
                tot = tot + kept[j]
            tot = tot.astype(F32)
            tgp[slot, i * 8 : (i + 1) * 8, :] = tot[:8] + tot[8:]
        for b in range(2):
            for k in range(2):
                at = (b * half + k * 8) * 8
                tot = tgp[slot, pl.ds(at, 8, stride=8), :]
                for s in range(1, 8):
                    tot = tot + tgp[slot, pl.ds(at + s, 8, stride=8), :]
                tg[dst + b, h, k] = tot

    def pick_copy(r, h, other):
        return pltpu.make_async_remote_copy(
            src_ref=tg.at[lax.rem(nt - r, nt), h, core + other * (1 - 2 * core)],
            dst_ref=tg_in.at[h, pl.ds(pl.multiple_of((core * nt + me) * 8, 8), 8)],
            send_sem=tg_ss.at[(h * nt + r) * 2 + other],
            recv_sem=tg_rs.at[(h * nt + r) * 2 + other],
            device_id=device(r, other),
            device_id_type=MESH,
        )

    def pick_step(n, c):
        h = n // 2
        first = (1 - lax.rem(n, 2)) * (nt // 2)
        pick_blocks(first + 2, h, 0)
        pick_blocks(first, h, 1)
        for b in range(nt // 2 - 1, 0, -1):
            for other in range(2):
                pick_copy(nt - first - b, h, other).start()
        pick_copy(lax.rem(nt - first, nt), h, 1).start()

        @pl.when(first > 0)
        def _():
            pick_copy(lax.rem(nt - first, nt), h, 0).start()

        return c

    lax.fori_loop(0, 4, pick_step, 0)

    mine = pl.ds(pl.multiple_of((core * nt + me) * 8, 8), 8)
    for h in range(2):
        tg_in[h, mine, :] = tg[0, h, core]

    def send_grad(target):
        return pltpu.make_async_remote_copy(
            src_ref=msg.at[target],
            dst_ref=pr.at[chip],
            send_sem=pr_ss,
            recv_sem=pr_rs,
            device_id={"path": target * 2 + core},
            device_id_type=MESH,
        )

    y, z = chip // ring, lax.rem(chip, ring)
    for h in range(2):
        for r in range(nt):
            for other in range(2):
                if r or other:
                    pick_copy(r, h, other).wait_recv()
        for c in range(half // 2):
            msg[c // quarter * ring + h * quarter + c % quarter] = jnp.concatenate(
                [tg_in[h, pl.ds(k * nt * 8 + c, nt, stride=8), :] for k in range(2)], axis=0
            ).astype(BF)
        for k in range(half // 2 - 1, 0, -1):
            to_z = h * quarter + lax.rem(z + k, quarter)
            send_grad(lax.rem(y + k // quarter, 2) * ring + to_z).start()
        same = y * ring + h * quarter + lax.rem(z, quarter)

        @pl.when(same != chip)
        def _():
            send_grad(same).start()

    pr[chip] = msg[chip]

    sibling.wait_recv()
    pairs = npath * nt
    ks = table_ref.shape[1]
    states = jnp.concatenate([st_in[k, c] for c in range(nchip) for k in range(2)], axis=0)
    hot = jnp.where(
        states == lax.broadcasted_iota(jnp.int32, (pairs, LANES), 1).astype(F32), 1.0, 0.0
    ).astype(BF)
    tab = jnp.concatenate(split3(table_ref[...].reshape(DATES * ks, LANES)), axis=0)
    at_date = lax.rem(
        lax.broadcasted_iota(jnp.int32, (3 * DATES * ks, pairs), 0) // ks, DATES
    )
    pair_date = lax.rem(
        lax.broadcasted_iota(jnp.int32, (3 * DATES * ks, pairs), 1), nt
    ) // per_date
    basis = jnp.where(
        at_date == pair_date, lax.dot_general(tab, hot, NT, preferred_element_type=F32), 0.0
    ).astype(BF)

    pltpu.make_async_copy(pr.at[others], pr.at[others], pr_rs).wait()
    total = jnp.dot(basis, pr[...].reshape(pairs, LANES), preferred_element_type=F32)
    total = total.reshape(3, DATES, ks, LANES)
    out_ref[...] = total[0] + total[1] + total[2]

    for r in range(1, nt):
        for copy in trade_copies(r):
            copy.wait_send()
    for r in range(nt):
        for other in range(2):
            if r or other:
                pick_copy(r, 0, other).wait_send()
                pick_copy(r, 1, other).wait_send()
    sibling.wait_send()
    pltpu.make_async_copy(st_in.at[core, others], st_in.at[core, others], st_ss).wait()
    pltpu.make_async_copy(pr.at[others], pr.at[others], pr_ss).wait()


def per_device(coef, set_ids, bucket_ids, states, table, risk_weight, correlation, date_weight):
    nt = lax.axis_size("trade")
    npath = lax.axis_size("path")
    trades = coef.shape[2]
    rows = trades // LANES
    nb = correlation.shape[0]
    wide = -(-nb // LANES) * LANES
    ks = table.shape[1]
    vmem = pl.BlockSpec(memory_space=pltpu.VMEM)
    hbm = pl.BlockSpec(memory_space=pltpu.HBM)
    dma = pltpu.SemaphoreType.DMA
    return pl.pallas_call(
        functools.partial(kernel, nt, npath),
        out_shape=pltpu.VMEM((DATES, ks, LANES), F32),
        in_specs=[hbm] * 8,
        out_specs=vmem,
        scratch_shapes=[
            pltpu.VMEM(coef.shape, F32),
            pltpu.VMEM((rows, LANES), jnp.int32),
            pltpu.VMEM((rows, LANES), jnp.int32),
            pltpu.SMEM(states.shape[::-1], jnp.int32),
            pltpu.VMEM(table.shape, F32),
            pltpu.VMEM((nb,), F32),
            pltpu.VMEM(correlation.shape, F32),
            pltpu.SMEM(date_weight.shape, F32),
            pltpu.VMEM((rows * 8, LANES), F32),
            pltpu.VMEM((nt, rows, LANES), BF),
            pltpu.VMEM((nt, rows, LANES), BF),
            pltpu.VMEM((nt, rows, LANES), jnp.int32),
            pltpu.VMEM((nt * rows, LANES), F32),
            pltpu.VMEM((nt * rows, LANES), F32),
            pltpu.VMEM((nt * rows, LANES), F32),
            pltpu.VMEM((HI, LO), F32),
            pltpu.VMEM((wide, wide), BF),
            pltpu.VMEM((wide, wide), BF),
            pltpu.VMEM((HI, LO), BF),
            pltpu.VMEM((2, rows * 8, LANES), F32),
            pltpu.VMEM((nt, 2, 2, 8, LANES), F32),
            pltpu.VMEM((2, 2 * nt * 8, LANES), F32),
            pltpu.VMEM((npath // 2, 2 * nt, LANES), BF),
            pltpu.VMEM((npath // 2, 2 * nt, LANES), BF),
            pltpu.VMEM((nt, LANES), F32),
            pltpu.VMEM((2, npath // 2, nt, LANES), F32),
            dma((7 + DATES,)),
            dma((nt,)),
            dma((nt,)),
            dma((nt,)),
            dma((nt,)),
            dma((4 * nt,)),
            dma((4 * nt,)),
            dma,
            dma,
            dma,
            dma,
            dma,
            dma,
        ],
        compiler_params=pltpu.CompilerParams(
            collective_id=0, has_side_effects=True, vmem_limit_bytes=48 * 1024 * 1024
        ),
    )(
        *(
            pltpu.with_memory_space_constraint(x, pltpu.HBM)
            for x in (
                coef,
                set_ids.reshape(rows, LANES),
                bucket_ids.reshape(rows, LANES),
                states.T,
                table,
                risk_weight,
                correlation,
                date_weight,
            )
        )
    )


def solution(mesh):
    in_specs = (P(None, None, "trade"), P("trade"), P("trade"), P(None, "path"), P(), P(), P(), P())
    out_specs = P(None, None, ("trade", "path"))
    return jax.shard_map(
        per_device, mesh=mesh, in_specs=in_specs, out_specs=out_specs, check_vma=False
    )
```

```python
import functools

import jax
import jax.numpy as jnp
from jax import lax
from jax.experimental import pallas as pl
from jax.experimental.pallas import tpu as pltpu
from jax.sharding import PartitionSpec as P

DATES = 4
SETS = 64
LO = 256
GROUPS = 3
HI = GROUPS * SETS
LANES = 128
MESH = pl.DeviceIdType.MESH
BF = jnp.bfloat16
F32 = jnp.float32
NT = (((1,), (1,)), ((), ()))


def split3(x):
    a = x.astype(BF)
    r = x - a.astype(F32)
    b = r.astype(BF)
    c = (r - b.astype(F32)).astype(BF)
    return a, b, c


def kernel(
    nt,
    npath,
    coef_hbm,
    set_hbm,
    bkt_hbm,
    st_hbm,
    table_hbm,
    rw_hbm,
    corr_hbm,
    dw_hbm,
    out_ref,
    coef_ref,
    set_ref,
    bkt_ref,
    st_ref,
    table_ref,
    rw_ref,
    corr_ref,
    dw_ref,
    part,
    sens_out,
    sens_in,
    cell_in,
    hi_f,
    lo_f,
    s_f,
    acc,
    chi,
    clo,
    grad,
    tgp,
    tg,
    tg_in,
    msg,
    pr,
    st_out,
    st_in,
    load_sem,
    sens_ss,
    sens_rs,
    cell_ss,
    cell_rs,
    tg_ss,
    tg_rs,
    st_ss,
    st_rs,
    sib_ss,
    sib_rs,
    pr_ss,
    pr_rs,
):
    me = lax.axis_index("trade")
    mp = lax.axis_index("path")
    core = lax.rem(mp, 2)
    chip = mp // 2
    nchip = npath // 2
    rows = set_ref.shape[0]
    half = rows // 2
    nb = corr_ref.shape[0]
    wide = chi.shape[0]
    per_date = nt // DATES
    ring = nchip // 2
    quarter = ring // 2

    def device(r, other):
        path = mp + other * (1 - 2 * core)
        return {"trade": lax.rem(me + r, nt), "path": path}

    def along(k):
        return {"path": lax.rem(chip + k, nchip) * 2 + core}

    loads = [
        pltpu.make_async_copy(src, dst, load_sem.at[i])
        for i, (src, dst) in enumerate(
            [
                (set_hbm, set_ref),
                (bkt_hbm, bkt_ref),
                (st_hbm, st_ref),
                (table_hbm, table_ref),
            ]
            + [(coef_hbm.at[d], coef_ref.at[d]) for d in range(DATES)]
            + [
                (corr_hbm, corr_ref),
                (rw_hbm, rw_ref),
                (dw_hbm, dw_ref),
            ]
        )
    ]
    for load in loads:
        load.start()

    barrier = pltpu.get_barrier_semaphore()
    for r in range(nt):
        for other in range(2):
            if r or other:
                pl.semaphore_signal(
                    barrier, inc=1, device_id=device(r, other), device_id_type=MESH
                )

    def greet(k, c):
        pl.semaphore_signal(barrier, inc=1, device_id=along(k), device_id_type=MESH)
        return c

    lax.fori_loop(1, nchip, greet, 0)

    def place(c):
        y, z, k = c // (2 * ring), c // 2 % ring, c % 2
        return ((z // quarter * 2 + k) * 2 + y) * quarter + z % quarter

    loads[0].wait()
    loads[1].wait()
    for c in range(rows):
        if c // 2 % quarter == 0:
            every = pl.ds(c, quarter, stride=2)
            bkt = bkt_ref[every, :]
            group = (bkt >= LO).astype(jnp.int32) + (bkt >= 2 * LO).astype(jnp.int32)
            cell_in[0, place(c) : place(c) + quarter, :] = (
                (group * SETS + set_ref[every, :]) * LO + bkt - group * LO
            )

    def trade_copies(r):
        return (
            pltpu.make_async_remote_copy(
                src_ref=cell_in.at[0],
                dst_ref=cell_in.at[r],
                send_sem=cell_ss,
                recv_sem=cell_rs,
                device_id=device(r, 0),
                device_id_type=MESH,
            ),
            pltpu.make_async_remote_copy(
                src_ref=sens_out.at[r],
                dst_ref=sens_in.at[r],
                send_sem=sens_ss,
                recv_sem=sens_rs,
                device_id=device(r, 0),
                device_id_type=MESH,
            ),
        )

    far = sorted(range(nt), key=lambda r: -min(r, nt - r))

    for load in loads[2 : 4 + DATES]:
        load.wait()
    lane = lax.broadcasted_iota(jnp.int32, table_ref.shape[1:], 1)
    for r in far:
        q = lax.rem(me + r, nt)
        d = q // per_date
        state = st_ref[lax.rem(q, per_date), d]
        col = jnp.sum(jnp.where(lane == state, table_ref[d], 0.0), axis=1, keepdims=True)
        for c in range(rows):
            x = coef_ref[d, :, c * LANES : (c + 1) * LANES] * col
            at = place(c)
            part[at * 8 : (at + 1) * 8, :] = x[:8] + x[8:]
        tots = []
        for g in range(rows // 8):
            tot = part[pl.ds(g * 64, 8, stride=8), :]
            for s in range(1, 8):
                tot = tot + part[pl.ds(g * 64 + s, 8, stride=8), :]
            tots.append(tot)
        if r:
            sens_out[r] = jnp.concatenate(tots, axis=0).astype(BF)
        else:
            sens_in[0] = jnp.concatenate(tots, axis=0).astype(BF)

    pl.semaphore_wait(barrier, 2 * nt - 1 + nchip - 1)
    for r in far[:-1]:
        for copy in trade_copies(r):
            copy.start()

    for d in range(DATES):
        for p in range(per_date):
            q = d * per_date + p
            st_out[q : q + 1, :] = jnp.full((1, LANES), st_ref[p, d], jnp.int32).astype(F32)

    def send_state(k, c):
        pltpu.make_async_remote_copy(
            src_ref=st_out,
            dst_ref=st_in.at[core, chip],
            send_sem=st_ss,
            recv_sem=st_rs,
            device_id=along(k),
            device_id_type=MESH,
        ).start()
        return c

    lax.fori_loop(1, nchip, send_state, 0)
    st_in[core, chip] = st_out[...]
    others = pl.ds(0, nchip - 1)
    sibling = pltpu.make_async_remote_copy(
        src_ref=st_in.at[core],
        dst_ref=st_in.at[core],
        send_sem=sib_ss,
        recv_sem=sib_rs,
        device_id=device(0, 1),
        device_id_type=MESH,
    )

    loads[4 + DATES].wait()
    chi[...] = jnp.zeros_like(chi)
    clo[...] = jnp.zeros_like(clo)
    corr = corr_ref[...]
    top = corr.astype(BF)
    chi[0:nb, 0:nb] = top
    clo[0:nb, 0:nb] = (corr - top.astype(F32)).astype(BF)

    hi_iota = lax.broadcasted_iota(jnp.int32, (HI, LANES), 0).astype(F32).astype(BF)
    lo_iota = lax.broadcasted_iota(jnp.int32, (LO, LANES), 0).astype(F32).astype(BF)
    lo_lane = lax.broadcasted_iota(jnp.int32, (LANES, LO), 1).astype(F32).astype(BF)
    one, zero = jnp.ones((), BF), jnp.zeros((), BF)

    def spread(ref, row, n):
        x = jnp.broadcast_to(ref[pl.ds(row, 1), :], (16, LANES)).astype(BF)
        return jnp.broadcast_to(x[None], (n // 16, 16, LANES)).reshape(n, LANES)

    def net_block(src):
        base = src * rows
        cells = cell_in[src]
        h = lax.shift_right_logical(cells, 8)
        low = (cells - h * LO).astype(F32)
        hi_f[base : base + rows, :] = h.astype(F32)
        lo_f[base : base + rows, :] = low
        s_f[base : base + rows, :] = sens_in[src].astype(F32)
        column = low.T.astype(BF)
        left, right = [], []
        for i in range(rows):
            left.append(
                jnp.where(
                    spread(hi_f, base + i, HI) == hi_iota, spread(s_f, base + i, HI), zero
                )
            )
            right.append(
                jnp.where(
                    jnp.broadcast_to(column[:, i : i + 1], (LANES, LO)) == lo_lane, one, zero
                )
            )
        return jnp.dot(
            jnp.concatenate(left, axis=1),
            jnp.concatenate(right, axis=0),
            preferred_element_type=F32,
        )

    acc[...] = net_block(0)

    def wait_all(ref, sem):
        pltpu.make_async_copy(ref, ref, sem).wait()

    received = pl.ds(1, nt - 1)
    wait_all(cell_in.at[received], cell_rs)
    wait_all(sens_in.at[received], sens_rs)

    total = acc[...]
    for r in range(1, nt):
        total = total + net_block(r)
    acc[...] = total

    pltpu.make_async_copy(st_in.at[core, others], st_in.at[core, others], st_rs).wait()
    sibling.start()

    loads[5 + DATES].wait()
    loads[6 + DATES].wait()
    rw = jnp.concatenate(
        [rw_ref[...].reshape(1, nb), jnp.zeros((1, wide - nb), F32)], axis=1
    )
    netted = jnp.concatenate(
        [
            acc[g * SETS : (g + 1) * SETS, : min(LO, wide - g * LO)]
            for g in range(GROUPS)
        ],
        axis=1,
    )
    w = netted * rw
    w_hi = w.astype(BF)
    w_lo = (w - w_hi.astype(F32)).astype(BF)
    both = jnp.dot(
        jnp.concatenate([w_hi, w_lo], axis=0), chi[...], preferred_element_type=F32
    )
    cw = both[:SETS] + both[SETS:] + jnp.dot(w_hi, clo[...], preferred_element_type=F32)
    margin = jnp.sqrt(jnp.sum(w * cw, axis=1, keepdims=True) + 1.0)
    weight = dw_ref[me // per_date]
    net_grad = ((weight * rw) * cw / margin).astype(BF)
    for g in range(GROUPS):
        part_g = net_grad[:, g * LO : min((g + 1) * LO, wide)]
        grad[g * SETS : (g + 1) * SETS, : part_g.shape[1]] = part_g
    grad[(GROUPS - 1) * SETS :, wide - (GROUPS - 1) * LO :] = jnp.zeros(
        (SETS, GROUPS * LO - wide), BF
    )

    def pick_blocks(dst, h, slot):
        def row(i):
            return pl.multiple_of(dst * rows + h * half, half) + i // half * rows + i % half

        right = jnp.concatenate(
            [
                jnp.where(spread(lo_f, row(i), LO) == lo_iota, one, zero)
                for i in range(rows)
            ],
            axis=1,
        )
        product = jnp.dot(grad[...], right, preferred_element_type=F32).astype(BF)
        for i in range(rows):
            kept = jnp.where(
                spread(hi_f, row(i), HI) == hi_iota,
                product[:, i * LANES : (i + 1) * LANES],
                zero,
            ).reshape(HI // 16, 16, LANES)
            tot = kept[0]
            for j in range(1, HI // 16):
                tot = tot + kept[j]
            tot = tot.astype(F32)
            tgp[slot, i * 8 : (i + 1) * 8, :] = tot[:8] + tot[8:]
        for b in range(2):
            for k in range(2):
                at = (b * half + k * 8) * 8
                tot = tgp[slot, pl.ds(at, 8, stride=8), :]
                for s in range(1, 8):
                    tot = tot + tgp[slot, pl.ds(at + s, 8, stride=8), :]
                tg[dst + b, h, k] = tot

    def pick_copy(r, h, other):
        return pltpu.make_async_remote_copy(
            src_ref=tg.at[lax.rem(nt - r, nt), h, core + other * (1 - 2 * core)],
            dst_ref=tg_in.at[h, pl.ds(pl.multiple_of((core * nt + me) * 8, 8), 8)],
            send_sem=tg_ss.at[h],
            recv_sem=tg_rs.at[h],
            device_id=device(r, other),
            device_id_type=MESH,
        )

    def pick_step(n, c):
        h = n // 2
        first = (1 - lax.rem(n, 2)) * (nt // 2)
        pick_blocks(first + 2, h, 0)
        pick_blocks(first, h, 1)
        for b in range(nt // 2 - 1, 0, -1):
            for other in range(2):
                pick_copy(nt - first - b, h, other).start()
        pick_copy(lax.rem(nt - first, nt), h, 1).start()

        @pl.when(first > 0)
        def _():
            pick_copy(lax.rem(nt - first, nt), h, 0).start()

        return c

    lax.fori_loop(0, 4, pick_step, 0)

    mine = pl.ds(pl.multiple_of((core * nt + me) * 8, 8), 8)
    for h in range(2):
        tg_in[h, mine, :] = tg[0, h, core]

    def send_grad(target):
        return pltpu.make_async_remote_copy(
            src_ref=msg.at[target],
            dst_ref=pr.at[chip],
            send_sem=pr_ss,
            recv_sem=pr_rs,
            device_id={"path": target * 2 + core},
            device_id_type=MESH,
        )

    y, z = chip // ring, lax.rem(chip, ring)
    for h in range(2):
        wait_all(tg_in.at[h, pl.ds(0, (2 * nt - 1) * 8)], tg_rs.at[h])
        for c in range(half // 2):
            msg[c // quarter * ring + h * quarter + c % quarter] = jnp.concatenate(
                [tg_in[h, pl.ds(k * nt * 8 + c, nt, stride=8), :] for k in range(2)], axis=0
            ).astype(BF)
        for k in range(half // 2 - 1, 0, -1):
            to_z = h * quarter + lax.rem(z + k, quarter)
            send_grad(lax.rem(y + k // quarter, 2) * ring + to_z).start()
        same = y * ring + h * quarter + lax.rem(z, quarter)

        @pl.when(same != chip)
        def _():
            send_grad(same).start()

    pr[chip] = msg[chip]

    sibling.wait_recv()
    pairs = npath * nt
    ks = table_ref.shape[1]
    states = jnp.concatenate([st_in[k, c] for c in range(nchip) for k in range(2)], axis=0)
    hot = jnp.where(
        states == lax.broadcasted_iota(jnp.int32, (pairs, LANES), 1).astype(F32), 1.0, 0.0
    ).astype(BF)
    tab = jnp.concatenate(split3(table_ref[...].reshape(DATES * ks, LANES)), axis=0)
    at_date = lax.rem(
        lax.broadcasted_iota(jnp.int32, (3 * DATES * ks, pairs), 0) // ks, DATES
    )
    pair_date = lax.rem(
        lax.broadcasted_iota(jnp.int32, (3 * DATES * ks, pairs), 1), nt
    ) // per_date
    basis = jnp.where(
        at_date == pair_date, lax.dot_general(tab, hot, NT, preferred_element_type=F32), 0.0
    ).astype(BF)

    wait_all(cell_in.at[received], cell_ss)
    wait_all(sens_in.at[received], sens_ss)
    wait_all(tg_in.at[0, pl.ds(0, (2 * nt - 1) * 8)], tg_ss.at[0])
    wait_all(tg_in.at[1, pl.ds(0, (2 * nt - 1) * 8)], tg_ss.at[1])
    sibling.wait_send()
    pltpu.make_async_copy(st_in.at[core, others], st_in.at[core, others], st_ss).wait()
    pltpu.make_async_copy(pr.at[others], pr.at[others], pr_rs).wait()
    total = jnp.dot(basis, pr[...].reshape(pairs, LANES), preferred_element_type=F32)
    total = total.reshape(3, DATES, ks, LANES)
    out_ref[...] = total[0] + total[1] + total[2]

    pltpu.make_async_copy(pr.at[others], pr.at[others], pr_ss).wait()


def per_device(coef, set_ids, bucket_ids, states, table, risk_weight, correlation, date_weight):
    nt = lax.axis_size("trade")
    npath = lax.axis_size("path")
    trades = coef.shape[2]
    rows = trades // LANES
    nb = correlation.shape[0]
    wide = -(-nb // LANES) * LANES
    ks = table.shape[1]
    vmem = pl.BlockSpec(memory_space=pltpu.VMEM)
    hbm = pl.BlockSpec(memory_space=pltpu.HBM)
    dma = pltpu.SemaphoreType.DMA
    return pl.pallas_call(
        functools.partial(kernel, nt, npath),
        out_shape=pltpu.VMEM((DATES, ks, LANES), F32),
        in_specs=[hbm] * 8,
        out_specs=vmem,
        scratch_shapes=[
            pltpu.VMEM(coef.shape, F32),
            pltpu.VMEM((rows, LANES), jnp.int32),
            pltpu.VMEM((rows, LANES), jnp.int32),
            pltpu.SMEM(states.shape[::-1], jnp.int32),
            pltpu.VMEM(table.shape, F32),
            pltpu.VMEM((nb,), F32),
            pltpu.VMEM(correlation.shape, F32),
            pltpu.SMEM(date_weight.shape, F32),
            pltpu.VMEM((rows * 8, LANES), F32),
            pltpu.VMEM((nt, rows, LANES), BF),
            pltpu.VMEM((nt, rows, LANES), BF),
            pltpu.VMEM((nt, rows, LANES), jnp.int32),
            pltpu.VMEM((nt * rows, LANES), F32),
            pltpu.VMEM((nt * rows, LANES), F32),
            pltpu.VMEM((nt * rows, LANES), F32),
            pltpu.VMEM((HI, LO), F32),
            pltpu.VMEM((wide, wide), BF),
            pltpu.VMEM((wide, wide), BF),
            pltpu.VMEM((HI, LO), BF),
            pltpu.VMEM((2, rows * 8, LANES), F32),
            pltpu.VMEM((nt, 2, 2, 8, LANES), F32),
            pltpu.VMEM((2, 2 * nt * 8, LANES), F32),
            pltpu.VMEM((npath // 2, 2 * nt, LANES), BF),
            pltpu.VMEM((npath // 2, 2 * nt, LANES), BF),
            pltpu.VMEM((nt, LANES), F32),
            pltpu.VMEM((2, npath // 2, nt, LANES), F32),
            dma((7 + DATES,)),
            dma,
            dma,
            dma,
            dma,
            dma((2,)),
            dma((2,)),
            dma,
            dma,
            dma,
            dma,
            dma,
            dma,
        ],
        compiler_params=pltpu.CompilerParams(
            collective_id=0, has_side_effects=True, vmem_limit_bytes=48 * 1024 * 1024
        ),
    )(
        *(
            pltpu.with_memory_space_constraint(x, pltpu.HBM)
            for x in (
                coef,
                set_ids.reshape(rows, LANES),
                bucket_ids.reshape(rows, LANES),
                states.T,
                table,
                risk_weight,
                correlation,
                date_weight,
            )
        )
    )


def solution(mesh):
    in_specs = (P(None, None, "trade"), P("trade"), P("trade"), P(None, "path"), P(), P(), P(), P())
    out_specs = P(None, None, ("trade", "path"))
    return jax.shard_map(
        per_device, mesh=mesh, in_specs=in_specs, out_specs=out_specs, check_vma=False
    )
```

```python
import functools

import jax
import jax.numpy as jnp
from jax import lax
from jax.experimental import pallas as pl
from jax.experimental.pallas import tpu as pltpu
from jax.sharding import PartitionSpec as P

DATES = 4
SETS = 64
LO = 256
LANES = 128
MESH = pl.DeviceIdType.MESH
BF = jnp.bfloat16
F32 = jnp.float32
NT = (((1,), (1,)), ((), ()))


def split3(x):
    a = x.astype(BF)
    r = x - a.astype(F32)
    b = r.astype(BF)
    c = (r - b.astype(F32)).astype(BF)
    return a, b, c


def kernel(
    nt,
    npath,
    coef_hbm,
    set_hbm,
    bkt_hbm,
    st_hbm,
    table_hbm,
    rw_hbm,
    corr_hbm,
    dw_hbm,
    out_ref,
    coef_ref,
    set_ref,
    bkt_ref,
    st_ref,
    table_ref,
    rw_ref,
    corr_ref,
    dw_ref,
    part,
    sens_out,
    sens_in,
    cell_in,
    hi_f,
    lo_f,
    s_f,
    acc,
    chi,
    clo,
    gradf,
    grad,
    tgp,
    tg,
    tg_in,
    msg,
    pr,
    st_out,
    st_in,
    load_sem,
    sens_ss,
    sens_rs,
    cell_ss,
    cell_rs,
    tg_ss,
    tg_rs,
    st_ss,
    st_rs,
    sib_ss,
    sib_rs,
    pr_ss,
    pr_rs,
):
    me = lax.axis_index("trade")
    mp = lax.axis_index("path")
    core = lax.rem(mp, 2)
    chip = mp // 2
    nchip = npath // 2
    rows = set_ref.shape[0]
    half = rows // 2
    nb = corr_ref.shape[0]
    wide = chi.shape[0]
    hi_rows = grad.shape[0]
    tiles, per_row = wide // LANES, LO // LANES
    apart = SETS // per_row
    per_date = nt // DATES
    ring = nchip // 2
    quarter = ring // 2

    def device(r, other):
        path = mp + other * (1 - 2 * core)
        return {"trade": lax.rem(me + r, nt), "path": path}

    def along(k):
        return {"path": lax.rem(chip + k, nchip) * 2 + core}

    loads = [
        pltpu.make_async_copy(src, dst, load_sem.at[i])
        for i, (src, dst) in enumerate(
            [
                (set_hbm, set_ref),
                (bkt_hbm, bkt_ref),
                (st_hbm, st_ref),
                (table_hbm, table_ref),
            ]
            + [(coef_hbm.at[d], coef_ref.at[d]) for d in range(DATES)]
            + [
                (corr_hbm, corr_ref),
                (rw_hbm, rw_ref),
                (dw_hbm, dw_ref),
            ]
        )
    ]
    for load in loads:
        load.start()

    barrier = pltpu.get_barrier_semaphore()
    for r in range(nt):
        for other in range(2):
            if r or other:
                pl.semaphore_signal(
                    barrier, inc=1, device_id=device(r, other), device_id_type=MESH
                )

    def greet(k, c):
        pl.semaphore_signal(barrier, inc=1, device_id=along(k), device_id_type=MESH)
        return c

    lax.fori_loop(1, nchip, greet, 0)

    def place(c):
        y, z, k = c // (2 * ring), c // 2 % ring, c % 2
        return ((z // quarter * 2 + k) * 2 + y) * quarter + z % quarter

    loads[0].wait()
    loads[1].wait()
    for c in range(rows):
        if c // 2 % quarter == 0:
            every = pl.ds(c, quarter, stride=2)
            cell_in[0, place(c) : place(c) + quarter, :] = (
                set_ref[every, :] * wide + bkt_ref[every, :]
            )

    def trade_copies(r):
        return (
            pltpu.make_async_remote_copy(
                src_ref=cell_in.at[0],
                dst_ref=cell_in.at[r],
                send_sem=cell_ss,
                recv_sem=cell_rs,
                device_id=device(r, 0),
                device_id_type=MESH,
            ),
            pltpu.make_async_remote_copy(
                src_ref=sens_out.at[lax.rem(me + r, nt)],
                dst_ref=sens_in.at[r],
                send_sem=sens_ss,
                recv_sem=sens_rs,
                device_id=device(r, 0),
                device_id_type=MESH,
            ),
        )

    far = sorted(range(nt), key=lambda r: -min(r, nt - r))

    loads[2].wait()
    loads[3].wait()
    lane = lax.broadcasted_iota(jnp.int32, table_ref.shape[1:], 1)
    for q in range(nt):
        d = q // per_date
        if q % per_date == 0:
            loads[4 + d].wait()
        state = st_ref[q % per_date, d]
        col = jnp.sum(jnp.where(lane == state, table_ref[d], 0.0), axis=1, keepdims=True)
        for c in range(rows):
            x = coef_ref[d, :, c * LANES : (c + 1) * LANES] * col
            at = place(c)
            part[at * 8 : (at + 1) * 8, :] = x[:8] + x[8:]
        tots = []
        for g in range(rows // 8):
            tot = part[pl.ds(g * 64, 8, stride=8), :]
            for s in range(1, 8):
                tot = tot + part[pl.ds(g * 64 + s, 8, stride=8), :]
            tots.append(tot)
        sens_out[q] = jnp.concatenate(tots, axis=0).astype(BF)

    pl.semaphore_wait(barrier, 2 * nt - 1 + nchip - 1)
    for r in far[:-1]:
        for copy in trade_copies(r):
            copy.start()
    sens_in[0] = sens_out[me]

    for d in range(DATES):
        for p in range(per_date):
            q = d * per_date + p
            st_out[q : q + 1, :] = jnp.full((1, LANES), st_ref[p, d], jnp.int32).astype(F32)

    def send_state(k, c):
        pltpu.make_async_remote_copy(
            src_ref=st_out,
            dst_ref=st_in.at[core, chip],
            send_sem=st_ss,
            recv_sem=st_rs,
            device_id=along(k),
            device_id_type=MESH,
        ).start()
        return c

    lax.fori_loop(1, nchip, send_state, 0)
    st_in[core, chip] = st_out[...]
    others = pl.ds(0, nchip - 1)
    sibling = pltpu.make_async_remote_copy(
        src_ref=st_in.at[core],
        dst_ref=st_in.at[core],
        send_sem=sib_ss,
        recv_sem=sib_rs,
        device_id=device(0, 1),
        device_id_type=MESH,
    )

    loads[4 + DATES].wait()
    chi[...] = jnp.zeros_like(chi)
    clo[...] = jnp.zeros_like(clo)
    corr = corr_ref[...]
    top = corr.astype(BF)
    chi[0:nb, 0:nb] = top
    clo[0:nb, 0:nb] = (corr - top.astype(F32)).astype(BF)

    hi_iota = lax.broadcasted_iota(jnp.int32, (hi_rows, LANES), 0).astype(F32).astype(BF)
    lo_iota = lax.broadcasted_iota(jnp.int32, (LO, LANES), 0).astype(F32).astype(BF)
    lo_lane = lax.broadcasted_iota(jnp.int32, (LANES, LO), 1).astype(F32).astype(BF)
    one, zero = jnp.ones((), BF), jnp.zeros((), BF)

    def spread(ref, row, n):
        x = jnp.broadcast_to(ref[pl.ds(row, 1), :], (16, LANES)).astype(BF)
        return jnp.broadcast_to(x[None], (n // 16, 16, LANES)).reshape(n, LANES)

    def net_block(src):
        base = src * rows
        cells = cell_in[src]
        h = lax.shift_right_logical(cells, 8)
        low = (cells - h * LO).astype(F32)
        hi_f[base : base + rows, :] = h.astype(F32)
        lo_f[base : base + rows, :] = low
        s_f[base : base + rows, :] = sens_in[src].astype(F32)
        column = low.T.astype(BF)
        left, right = [], []
        for i in range(rows):
            left.append(
                jnp.where(
                    spread(hi_f, base + i, hi_rows) == hi_iota, spread(s_f, base + i, hi_rows), zero
                )
            )
            right.append(
                jnp.where(
                    jnp.broadcast_to(column[:, i : i + 1], (LANES, LO)) == lo_lane, one, zero
                )
            )
        return jnp.dot(
            jnp.concatenate(left, axis=1),
            jnp.concatenate(right, axis=0),
            preferred_element_type=F32,
        )

    def halves(x):
        for k in range(per_row):
            acc[k] = x[:, k * LANES : (k + 1) * LANES]

    halves(net_block(0))

    def wait_all(ref, sem):
        pltpu.make_async_copy(ref, ref, sem).wait()

    received = pl.ds(1, nt - 1)
    wait_all(cell_in.at[received], cell_rs)
    wait_all(sens_in.at[received], sens_rs)

    total = jnp.concatenate([acc[k] for k in range(per_row)], axis=1)
    for r in range(1, nt):
        total = total + net_block(r)
    halves(total)

    pltpu.make_async_copy(st_in.at[core, others], st_in.at[core, others], st_rs).wait()
    sibling.start()

    loads[5 + DATES].wait()
    loads[6 + DATES].wait()
    rw = jnp.concatenate(
        [rw_ref[...].reshape(1, nb), jnp.zeros((1, wide - nb), F32)], axis=1
    )
    def tile(rest, j):
        at = rest * tiles + j
        return at % per_row, pl.ds(at // per_row, apart, stride=tiles)

    def tile_of(ref, rest, j):
        half_row, every = tile(rest, j)
        return ref[half_row, every, :]

    netted = jnp.concatenate(
        [
            jnp.concatenate([tile_of(acc, rest, j) for j in range(tiles)], axis=1)
            for rest in range(per_row)
        ],
        axis=0,
    )
    w = netted * rw
    w_hi = w.astype(BF)
    w_lo = (w - w_hi.astype(F32)).astype(BF)
    both = jnp.dot(
        jnp.concatenate([w_hi, w_lo], axis=0), chi[...], preferred_element_type=F32
    )
    cw = both[:SETS] + both[SETS:] + jnp.dot(w_hi, clo[...], preferred_element_type=F32)
    margin = jnp.sqrt(jnp.sum(w * cw, axis=1, keepdims=True) + 1.0)
    weight = dw_ref[me // per_date]
    net_grad = (weight * rw) * cw / margin
    for rest in range(per_row):
        for j in range(tiles):
            half_row, every = tile(rest, j)
            gradf[half_row, every, :] = net_grad[
                rest * apart : (rest + 1) * apart, j * LANES : (j + 1) * LANES
            ]
    grad[...] = jnp.concatenate([gradf[k] for k in range(per_row)], axis=1).astype(BF)

    def pick_blocks(dst, h, slot):
        def row(i):
            return pl.multiple_of(dst * rows + h * half, half) + i // half * rows + i % half

        right = jnp.concatenate(
            [
                jnp.where(spread(lo_f, row(i), LO) == lo_iota, one, zero)
                for i in range(rows)
            ],
            axis=1,
        )
        product = jnp.dot(grad[...], right, preferred_element_type=F32).astype(BF)
        for i in range(rows):
            kept = jnp.where(
                spread(hi_f, row(i), hi_rows) == hi_iota,
                product[:, i * LANES : (i + 1) * LANES],
                zero,
            ).reshape(hi_rows // 16, 16, LANES)
            tot = kept[0]
            for j in range(1, hi_rows // 16):
                tot = tot + kept[j]
            tot = tot.astype(F32)
            tgp[slot, i * 8 : (i + 1) * 8, :] = tot[:8] + tot[8:]
        for b in range(2):
            for k in range(2):
                at = (b * half + k * 8) * 8
                tot = tgp[slot, pl.ds(at, 8, stride=8), :]
                for s in range(1, 8):
                    tot = tot + tgp[slot, pl.ds(at + s, 8, stride=8), :]
                tg[dst + b, h, k] = tot

    def pick_copy(r, h, other):
        return pltpu.make_async_remote_copy(
            src_ref=tg.at[lax.rem(nt - r, nt), h, core + other * (1 - 2 * core)],
            dst_ref=tg_in.at[h, pl.ds(pl.multiple_of((core * nt + me) * 8, 8), 8)],
            send_sem=tg_ss.at[h],
            recv_sem=tg_rs.at[h],
            device_id=device(r, other),
            device_id_type=MESH,
        )

    def pick_step(n, c):
        h = n // 2
        first = (1 - lax.rem(n, 2)) * (nt // 2)
        pick_blocks(first + 2, h, 0)
        pick_blocks(first, h, 1)
        for b in range(nt // 2 - 1, 0, -1):
            for other in range(2):
                pick_copy(nt - first - b, h, other).start()
        pick_copy(lax.rem(nt - first, nt), h, 1).start()

        @pl.when(first > 0)
        def _():
            pick_copy(lax.rem(nt - first, nt), h, 0).start()

        return c

    lax.fori_loop(0, 4, pick_step, 0)

    mine = pl.ds(pl.multiple_of((core * nt + me) * 8, 8), 8)
    for h in range(2):
        tg_in[h, mine, :] = tg[0, h, core]

    def send_grad(target):
        return pltpu.make_async_remote_copy(
            src_ref=msg.at[target],
            dst_ref=pr.at[chip],
            send_sem=pr_ss,
            recv_sem=pr_rs,
            device_id={"path": target * 2 + core},
            device_id_type=MESH,
        )

    y, z = chip // ring, lax.rem(chip, ring)
    for h in range(2):
        wait_all(tg_in.at[h, pl.ds(0, (2 * nt - 1) * 8)], tg_rs.at[h])
        for c in range(half // 2):
            msg[c // quarter * ring + h * quarter + c % quarter] = jnp.concatenate(
                [tg_in[h, pl.ds(k * nt * 8 + c, nt, stride=8), :] for k in range(2)], axis=0
            ).astype(BF)
        for k in range(half // 2 - 1, 0, -1):
            to_z = h * quarter + lax.rem(z + k, quarter)
            send_grad(lax.rem(y + k // quarter, 2) * ring + to_z).start()
        same = y * ring + h * quarter + lax.rem(z, quarter)

        @pl.when(same != chip)
        def _():
            send_grad(same).start()

    pr[chip] = msg[chip]

    sibling.wait_recv()
    pairs = npath * nt
    ks = table_ref.shape[1]
    states = jnp.concatenate([st_in[k, c] for c in range(nchip) for k in range(2)], axis=0)
    hot = jnp.where(
        states == lax.broadcasted_iota(jnp.int32, (pairs, LANES), 1).astype(F32), 1.0, 0.0
    ).astype(BF)
    tab = jnp.concatenate(split3(table_ref[...].reshape(DATES * ks, LANES)), axis=0)
    at_date = lax.rem(
        lax.broadcasted_iota(jnp.int32, (3 * DATES * ks, pairs), 0) // ks, DATES
    )
    pair_date = lax.rem(
        lax.broadcasted_iota(jnp.int32, (3 * DATES * ks, pairs), 1), nt
    ) // per_date
    basis = jnp.where(
        at_date == pair_date, lax.dot_general(tab, hot, NT, preferred_element_type=F32), 0.0
    ).astype(BF)

    wait_all(cell_in.at[received], cell_ss)
    wait_all(sens_in.at[received], sens_ss)
    wait_all(tg_in.at[0, pl.ds(0, (2 * nt - 1) * 8)], tg_ss.at[0])
    wait_all(tg_in.at[1, pl.ds(0, (2 * nt - 1) * 8)], tg_ss.at[1])
    sibling.wait_send()
    pltpu.make_async_copy(st_in.at[core, others], st_in.at[core, others], st_ss).wait()
    pltpu.make_async_copy(pr.at[others], pr.at[others], pr_rs).wait()
    total = jnp.dot(basis, pr[...].reshape(pairs, LANES), preferred_element_type=F32)
    total = total.reshape(3, DATES, ks, LANES)
    out_ref[...] = total[0] + total[1] + total[2]

    pltpu.make_async_copy(pr.at[others], pr.at[others], pr_ss).wait()


def per_device(coef, set_ids, bucket_ids, states, table, risk_weight, correlation, date_weight):
    nt = lax.axis_size("trade")
    npath = lax.axis_size("path")
    trades = coef.shape[2]
    rows = trades // LANES
    nb = correlation.shape[0]
    wide = -(-nb // LANES) * LANES
    hi_rows = SETS * wide // LO
    ks = table.shape[1]
    vmem = pl.BlockSpec(memory_space=pltpu.VMEM)
    hbm = pl.BlockSpec(memory_space=pltpu.HBM)
    dma = pltpu.SemaphoreType.DMA
    return pl.pallas_call(
        functools.partial(kernel, nt, npath),
        out_shape=pltpu.VMEM((DATES, ks, LANES), F32),
        in_specs=[hbm] * 8,
        out_specs=vmem,
        scratch_shapes=[
            pltpu.VMEM(coef.shape, F32),
            pltpu.VMEM((rows, LANES), jnp.int32),
            pltpu.VMEM((rows, LANES), jnp.int32),
            pltpu.SMEM(states.shape[::-1], jnp.int32),
            pltpu.VMEM(table.shape, F32),
            pltpu.VMEM((nb,), F32),
            pltpu.VMEM(correlation.shape, F32),
            pltpu.SMEM(date_weight.shape, F32),
            pltpu.VMEM((rows * 8, LANES), F32),
            pltpu.VMEM((nt, rows, LANES), BF),
            pltpu.VMEM((nt, rows, LANES), BF),
            pltpu.VMEM((nt, rows, LANES), jnp.int32),
            pltpu.VMEM((nt * rows, LANES), F32),
            pltpu.VMEM((nt * rows, LANES), F32),
            pltpu.VMEM((nt * rows, LANES), F32),
            pltpu.VMEM((LO // LANES, hi_rows, LANES), F32),
            pltpu.VMEM((wide, wide), BF),
            pltpu.VMEM((wide, wide), BF),
            pltpu.VMEM((LO // LANES, hi_rows, LANES), F32),
            pltpu.VMEM((hi_rows, LO), BF),
            pltpu.VMEM((2, rows * 8, LANES), F32),
            pltpu.VMEM((nt, 2, 2, 8, LANES), F32),
            pltpu.VMEM((2, 2 * nt * 8, LANES), F32),
            pltpu.VMEM((npath // 2, 2 * nt, LANES), BF),
            pltpu.VMEM((npath // 2, 2 * nt, LANES), BF),
            pltpu.VMEM((nt, LANES), F32),
            pltpu.VMEM((2, npath // 2, nt, LANES), F32),
            dma((7 + DATES,)),
            dma,
            dma,
            dma,
            dma,
            dma((2,)),
            dma((2,)),
            dma,
            dma,
            dma,
            dma,
            dma,
            dma,
        ],
        compiler_params=pltpu.CompilerParams(
            collective_id=0, has_side_effects=True, vmem_limit_bytes=48 * 1024 * 1024
        ),
    )(
        *(
            pltpu.with_memory_space_constraint(x, pltpu.HBM)
            for x in (
                coef,
                set_ids.reshape(rows, LANES),
                bucket_ids.reshape(rows, LANES),
                states.T,
                table,
                risk_weight,
                correlation,
                date_weight,
            )
        )
    )


def solution(mesh):
    in_specs = (P(None, None, "trade"), P("trade"), P("trade"), P(None, "path"), P(), P(), P(), P())
    out_specs = P(None, None, ("trade", "path"))
    return jax.shard_map(
        per_device, mesh=mesh, in_specs=in_specs, out_specs=out_specs, check_vma=False
    )
```

```python
import functools

import jax
import jax.numpy as jnp
from jax import lax
from jax.experimental import pallas as pl
from jax.experimental.pallas import tpu as pltpu
from jax.sharding import PartitionSpec as P

DATES = 4
SETS = 64
LO = 256
LANES = 128
MESH = pl.DeviceIdType.MESH
BF = jnp.bfloat16
F32 = jnp.float32
NT = (((1,), (1,)), ((), ()))


def split3(x):
    a = x.astype(BF)
    r = x - a.astype(F32)
    b = r.astype(BF)
    c = (r - b.astype(F32)).astype(BF)
    return a, b, c


def kernel(
    nt,
    npath,
    coef_hbm,
    set_hbm,
    bkt_hbm,
    st_hbm,
    table_hbm,
    rw_hbm,
    corr_hbm,
    dw_hbm,
    out_ref,
    coef_ref,
    set_ref,
    bkt_ref,
    st_ref,
    table_ref,
    rw_ref,
    corr_ref,
    dw_ref,
    part,
    sens_out,
    sens_in,
    cell_in,
    hi_f,
    lo_f,
    s_f,
    acc,
    chi,
    cmid,
    clo,
    gradf,
    grad,
    tgp,
    tg,
    tg_in,
    msg,
    pr,
    st_out,
    st_in,
    load_sem,
    sens_ss,
    sens_rs,
    cell_ss,
    cell_rs,
    tg_ss,
    tg_rs,
    st_ss,
    st_rs,
    sib_ss,
    sib_rs,
    pr_ss,
    pr_rs,
):
    me = lax.axis_index("trade")
    mp = lax.axis_index("path")
    core = lax.rem(mp, 2)
    chip = mp // 2
    nchip = npath // 2
    rows = set_ref.shape[0]
    half = rows // 2
    nb = corr_ref.shape[0]
    wide = chi.shape[0]
    hi_rows = grad.shape[0]
    tiles, per_row = wide // LANES, LO // LANES
    apart = SETS // per_row
    per_date = nt // DATES
    ring = nchip // 2
    quarter = ring // 2

    def device(r, other):
        path = mp + other * (1 - 2 * core)
        return {"trade": lax.rem(me + r, nt), "path": path}

    def along(k):
        return {"path": lax.rem(chip + k, nchip) * 2 + core}

    loads = [
        pltpu.make_async_copy(src, dst, load_sem.at[i])
        for i, (src, dst) in enumerate(
            [
                (set_hbm, set_ref),
                (bkt_hbm, bkt_ref),
                (st_hbm, st_ref),
                (table_hbm, table_ref),
            ]
            + [(coef_hbm.at[d], coef_ref.at[d]) for d in range(DATES)]
            + [
                (corr_hbm, corr_ref),
                (rw_hbm, rw_ref),
                (dw_hbm, dw_ref),
            ]
        )
    ]
    for load in loads:
        load.start()

    barrier = pltpu.get_barrier_semaphore()
    for r in range(nt):
        for other in range(2):
            if r or other:
                pl.semaphore_signal(
                    barrier, inc=1, device_id=device(r, other), device_id_type=MESH
                )

    def greet(k, c):
        pl.semaphore_signal(barrier, inc=1, device_id=along(k), device_id_type=MESH)
        return c

    lax.fori_loop(1, nchip, greet, 0)

    def place(c):
        y, z, k = c // (2 * ring), c // 2 % ring, c % 2
        return ((z // quarter * 2 + k) * 2 + y) * quarter + z % quarter

    loads[0].wait()
    loads[1].wait()
    for c in range(rows):
        if c // 2 % quarter == 0:
            every = pl.ds(c, quarter, stride=2)
            cell_in[0, place(c) : place(c) + quarter, :] = (
                set_ref[every, :] * wide + bkt_ref[every, :]
            )

    def trade_copies(r):
        return (
            pltpu.make_async_remote_copy(
                src_ref=cell_in.at[0],
                dst_ref=cell_in.at[r],
                send_sem=cell_ss,
                recv_sem=cell_rs,
                device_id=device(r, 0),
                device_id_type=MESH,
            ),
            pltpu.make_async_remote_copy(
                src_ref=sens_out.at[lax.rem(me + r, nt)],
                dst_ref=sens_in.at[r],
                send_sem=sens_ss,
                recv_sem=sens_rs,
                device_id=device(r, 0),
                device_id_type=MESH,
            ),
        )

    far = sorted(range(nt), key=lambda r: -min(r, nt - r))

    loads[2].wait()
    loads[3].wait()
    lane = lax.broadcasted_iota(jnp.int32, table_ref.shape[1:], 1)
    for q in range(nt):
        d = q // per_date
        if q % per_date == 0:
            loads[4 + d].wait()
        state = st_ref[q % per_date, d]
        col = jnp.sum(jnp.where(lane == state, table_ref[d], 0.0), axis=1, keepdims=True)
        for c in range(rows):
            x = coef_ref[d, :, c * LANES : (c + 1) * LANES] * col
            at = place(c)
            part[at * 8 : (at + 1) * 8, :] = x[:8] + x[8:]
        tots = []
        for g in range(rows // 8):
            tot = part[pl.ds(g * 64, 8, stride=8), :]
            for s in range(1, 8):
                tot = tot + part[pl.ds(g * 64 + s, 8, stride=8), :]
            tots.append(tot)
        sens_out[q] = jnp.concatenate(tots, axis=0).astype(BF)

    pl.semaphore_wait(barrier, 2 * nt - 1 + nchip - 1)
    for r in far[:-1]:
        for copy in trade_copies(r):
            copy.start()
    sens_in[0] = sens_out[me]

    for d in range(DATES):
        for p in range(per_date):
            q = d * per_date + p
            st_out[q : q + 1, :] = jnp.full((1, LANES), st_ref[p, d], jnp.int32).astype(F32)

    def send_state(k, c):
        pltpu.make_async_remote_copy(
            src_ref=st_out,
            dst_ref=st_in.at[core, chip],
            send_sem=st_ss,
            recv_sem=st_rs,
            device_id=along(k),
            device_id_type=MESH,
        ).start()
        return c

    lax.fori_loop(1, nchip, send_state, 0)
    st_in[core, chip] = st_out[...]
    others = pl.ds(0, nchip - 1)
    sibling = pltpu.make_async_remote_copy(
        src_ref=st_in.at[core],
        dst_ref=st_in.at[core],
        send_sem=sib_ss,
        recv_sem=sib_rs,
        device_id=device(0, 1),
        device_id_type=MESH,
    )

    loads[4 + DATES].wait()
    terms = (chi, cmid, clo)
    for ref, term in zip(terms, split3(corr_ref[...])):
        below, beside = nb // 16 * 16, nb // LANES * LANES
        ref[below:, :] = jnp.zeros((wide - below, wide), BF)
        ref[:, beside:] = jnp.zeros((wide, wide - beside), BF)
        ref[0:nb, 0:nb] = term

    hi_iota = lax.broadcasted_iota(jnp.int32, (hi_rows, LANES), 0).astype(F32).astype(BF)
    lo_iota = lax.broadcasted_iota(jnp.int32, (LO, LANES), 0).astype(F32).astype(BF)
    lo_lane = lax.broadcasted_iota(jnp.int32, (LANES, LO), 1).astype(F32).astype(BF)
    one, zero = jnp.ones((), BF), jnp.zeros((), BF)

    def spread(ref, row, n):
        x = jnp.broadcast_to(ref[pl.ds(row, 1), :], (16, LANES)).astype(BF)
        return jnp.broadcast_to(x[None], (n // 16, 16, LANES)).reshape(n, LANES)

    def net_block(src):
        base = src * rows
        cells = cell_in[src]
        h = lax.shift_right_logical(cells, 8)
        low = (cells - h * LO).astype(F32)
        hi_f[base : base + rows, :] = h.astype(F32)
        lo_f[base : base + rows, :] = low
        s_f[base : base + rows, :] = sens_in[src].astype(F32)
        column = low.T.astype(BF)
        left, right = [], []
        for i in range(rows):
            left.append(
                jnp.where(
                    spread(hi_f, base + i, hi_rows) == hi_iota, spread(s_f, base + i, hi_rows), zero
                )
            )
            right.append(
                jnp.where(
                    jnp.broadcast_to(column[:, i : i + 1], (LANES, LO)) == lo_lane, one, zero
                )
            )
        return jnp.dot(
            jnp.concatenate(left, axis=1),
            jnp.concatenate(right, axis=0),
            preferred_element_type=F32,
        )

    def halves(x):
        for k in range(per_row):
            acc[k] = x[:, k * LANES : (k + 1) * LANES]

    halves(net_block(0))

    def wait_all(ref, sem):
        pltpu.make_async_copy(ref, ref, sem).wait()

    received = pl.ds(1, nt - 1)
    wait_all(cell_in.at[received], cell_rs)
    wait_all(sens_in.at[received], sens_rs)

    total = jnp.concatenate([acc[k] for k in range(per_row)], axis=1)
    for r in range(1, nt):
        total = total + net_block(r)
    halves(total)

    pltpu.make_async_copy(st_in.at[core, others], st_in.at[core, others], st_rs).wait()
    sibling.start()

    loads[5 + DATES].wait()
    loads[6 + DATES].wait()
    rw = jnp.concatenate(
        [rw_ref[...].reshape(1, nb), jnp.zeros((1, wide - nb), F32)], axis=1
    )
    def tile(rest, j):
        at = rest * tiles + j
        return at % per_row, pl.ds(at // per_row, apart, stride=tiles)

    def tile_of(ref, rest, j):
        half_row, every = tile(rest, j)
        return ref[half_row, every, :]

    netted = jnp.concatenate(
        [
            jnp.concatenate([tile_of(acc, rest, j) for j in range(tiles)], axis=1)
            for rest in range(per_row)
        ],
        axis=0,
    )
    w = netted * rw
    ws = split3(w)
    cw = jnp.zeros_like(w)
    for n in range(1, 4):
        stacked = jnp.dot(
            jnp.concatenate(ws[:n], axis=0), terms[3 - n][...], preferred_element_type=F32
        )
        for i in range(n - 1, -1, -1):
            cw = cw + stacked[i * SETS : (i + 1) * SETS]
    margin = jnp.sqrt(jnp.sum(w * cw, axis=1, keepdims=True) + 1.0)
    weight = dw_ref[me // per_date]
    net_grad = (weight * rw) * cw / margin
    for rest in range(per_row):
        for j in range(tiles):
            half_row, every = tile(rest, j)
            gradf[half_row, every, :] = net_grad[
                rest * apart : (rest + 1) * apart, j * LANES : (j + 1) * LANES
            ]
    grad[...] = jnp.concatenate([gradf[k] for k in range(per_row)], axis=1).astype(BF)

    def pick_blocks(dst, h, slot):
        def row(i):
            return pl.multiple_of(dst * rows + h * half, half) + i // half * rows + i % half

        right = jnp.concatenate(
            [
                jnp.where(spread(lo_f, row(i), LO) == lo_iota, one, zero)
                for i in range(rows)
            ],
            axis=1,
        )
        product = jnp.dot(grad[...], right, preferred_element_type=F32).astype(BF)
        for i in range(rows):
            kept = jnp.where(
                spread(hi_f, row(i), hi_rows) == hi_iota,
                product[:, i * LANES : (i + 1) * LANES],
                zero,
            ).reshape(hi_rows // 16, 16, LANES)
            tot = kept[0]
            for j in range(1, hi_rows // 16):
                tot = tot + kept[j]
            tot = tot.astype(F32)
            tgp[slot, i * 8 : (i + 1) * 8, :] = tot[:8] + tot[8:]
        for b in range(2):
            for k in range(2):
                at = (b * half + k * 8) * 8
                tot = tgp[slot, pl.ds(at, 8, stride=8), :]
                for s in range(1, 8):
                    tot = tot + tgp[slot, pl.ds(at + s, 8, stride=8), :]
                tg[dst + b, h, k] = tot

    def pick_copy(r, h, other):
        return pltpu.make_async_remote_copy(
            src_ref=tg.at[lax.rem(nt - r, nt), h, core + other * (1 - 2 * core)],
            dst_ref=tg_in.at[h, pl.ds(pl.multiple_of((core * nt + me) * 8, 8), 8)],
            send_sem=tg_ss.at[h],
            recv_sem=tg_rs.at[h],
            device_id=device(r, other),
            device_id_type=MESH,
        )

    def pick_step(n, c):
        h = n // 2
        first = (1 - lax.rem(n, 2)) * (nt // 2)
        pick_blocks(first + 2, h, 0)
        pick_blocks(first, h, 1)
        for b in range(nt // 2 - 1, 0, -1):
            for other in range(2):
                pick_copy(nt - first - b, h, other).start()
        pick_copy(lax.rem(nt - first, nt), h, 1).start()

        @pl.when(first > 0)
        def _():
            pick_copy(lax.rem(nt - first, nt), h, 0).start()

        return c

    lax.fori_loop(0, 4, pick_step, 0)

    mine = pl.ds(pl.multiple_of((core * nt + me) * 8, 8), 8)
    for h in range(2):
        tg_in[h, mine, :] = tg[0, h, core]

    def send_grad(target):
        return pltpu.make_async_remote_copy(
            src_ref=msg.at[target],
            dst_ref=pr.at[chip],
            send_sem=pr_ss,
            recv_sem=pr_rs,
            device_id={"path": target * 2 + core},
            device_id_type=MESH,
        )

    y, z = chip // ring, lax.rem(chip, ring)
    for h in range(2):
        wait_all(tg_in.at[h, pl.ds(0, (2 * nt - 1) * 8)], tg_rs.at[h])
        for c in range(half // 2):
            msg[c // quarter * ring + h * quarter + c % quarter] = jnp.concatenate(
                [tg_in[h, pl.ds(k * nt * 8 + c, nt, stride=8), :] for k in range(2)], axis=0
            ).astype(BF)
        for k in range(half // 2 - 1, 0, -1):
            to_z = h * quarter + lax.rem(z + k, quarter)
            send_grad(lax.rem(y + k // quarter, 2) * ring + to_z).start()
        same = y * ring + h * quarter + lax.rem(z, quarter)

        @pl.when(same != chip)
        def _():
            send_grad(same).start()

    pr[chip] = msg[chip]

    sibling.wait_recv()
    pairs = npath * nt
    ks = table_ref.shape[1]
    states = jnp.concatenate([st_in[k, c] for c in range(nchip) for k in range(2)], axis=0)
    hot = jnp.where(
        states == lax.broadcasted_iota(jnp.int32, (pairs, LANES), 1).astype(F32), 1.0, 0.0
    ).astype(BF)
    tab = jnp.concatenate(split3(table_ref[...].reshape(DATES * ks, LANES)), axis=0)
    at_date = lax.rem(
        lax.broadcasted_iota(jnp.int32, (3 * DATES * ks, pairs), 0) // ks, DATES
    )
    pair_date = lax.rem(
        lax.broadcasted_iota(jnp.int32, (3 * DATES * ks, pairs), 1), nt
    ) // per_date
    basis = jnp.where(
        at_date == pair_date, lax.dot_general(tab, hot, NT, preferred_element_type=F32), 0.0
    ).astype(BF)

    wait_all(cell_in.at[received], cell_ss)
    wait_all(sens_in.at[received], sens_ss)
    wait_all(tg_in.at[0, pl.ds(0, (2 * nt - 1) * 8)], tg_ss.at[0])
    wait_all(tg_in.at[1, pl.ds(0, (2 * nt - 1) * 8)], tg_ss.at[1])
    sibling.wait_send()
    pltpu.make_async_copy(st_in.at[core, others], st_in.at[core, others], st_ss).wait()
    pltpu.make_async_copy(pr.at[others], pr.at[others], pr_rs).wait()
    total = jnp.dot(basis, pr[...].reshape(pairs, LANES), preferred_element_type=F32)
    total = total.reshape(3, DATES, ks, LANES)
    out_ref[...] = total[0] + total[1] + total[2]

    pltpu.make_async_copy(pr.at[others], pr.at[others], pr_ss).wait()


def per_device(coef, set_ids, bucket_ids, states, table, risk_weight, correlation, date_weight):
    nt = lax.axis_size("trade")
    npath = lax.axis_size("path")
    trades = coef.shape[2]
    rows = trades // LANES
    nb = correlation.shape[0]
    wide = -(-nb // LANES) * LANES
    hi_rows = SETS * wide // LO
    ks = table.shape[1]
    vmem = pl.BlockSpec(memory_space=pltpu.VMEM)
    hbm = pl.BlockSpec(memory_space=pltpu.HBM)
    dma = pltpu.SemaphoreType.DMA
    return pl.pallas_call(
        functools.partial(kernel, nt, npath),
        out_shape=pltpu.VMEM((DATES, ks, LANES), F32),
        in_specs=[hbm] * 8,
        out_specs=vmem,
        scratch_shapes=[
            pltpu.VMEM(coef.shape, F32),
            pltpu.VMEM((rows, LANES), jnp.int32),
            pltpu.VMEM((rows, LANES), jnp.int32),
            pltpu.SMEM(states.shape[::-1], jnp.int32),
            pltpu.VMEM(table.shape, F32),
            pltpu.VMEM((nb,), F32),
            pltpu.VMEM(correlation.shape, F32),
            pltpu.SMEM(date_weight.shape, F32),
            pltpu.VMEM((rows * 8, LANES), F32),
            pltpu.VMEM((nt, rows, LANES), BF),
            pltpu.VMEM((nt, rows, LANES), BF),
            pltpu.VMEM((nt, rows, LANES), jnp.int32),
            pltpu.VMEM((nt * rows, LANES), F32),
            pltpu.VMEM((nt * rows, LANES), F32),
            pltpu.VMEM((nt * rows, LANES), F32),
            pltpu.VMEM((LO // LANES, hi_rows, LANES), F32),
            pltpu.VMEM((wide, wide), BF),
            pltpu.VMEM((wide, wide), BF),
            pltpu.VMEM((wide, wide), BF),
            pltpu.VMEM((LO // LANES, hi_rows, LANES), F32),
            pltpu.VMEM((hi_rows, LO), BF),
            pltpu.VMEM((2, rows * 8, LANES), F32),
            pltpu.VMEM((nt, 2, 2, 8, LANES), F32),
            pltpu.VMEM((2, 2 * nt * 8, LANES), F32),
            pltpu.VMEM((npath // 2, 2 * nt, LANES), BF),
            pltpu.VMEM((npath // 2, 2 * nt, LANES), BF),
            pltpu.VMEM((nt, LANES), F32),
            pltpu.VMEM((2, npath // 2, nt, LANES), F32),
            dma((7 + DATES,)),
            dma,
            dma,
            dma,
            dma,
            dma((2,)),
            dma((2,)),
            dma,
            dma,
            dma,
            dma,
            dma,
            dma,
        ],
        compiler_params=pltpu.CompilerParams(
            collective_id=0, has_side_effects=True, vmem_limit_bytes=48 * 1024 * 1024
        ),
    )(
        *(
            pltpu.with_memory_space_constraint(x, pltpu.HBM)
            for x in (
                coef,
                set_ids.reshape(rows, LANES),
                bucket_ids.reshape(rows, LANES),
                states.T,
                table,
                risk_weight,
                correlation,
                date_weight,
            )
        )
    )


def solution(mesh):
    in_specs = (P(None, None, "trade"), P("trade"), P("trade"), P(None, "path"), P(), P(), P(), P())
    out_specs = P(None, None, ("trade", "path"))
    return jax.shard_map(
        per_device, mesh=mesh, in_specs=in_specs, out_specs=out_specs, check_vma=False
    )
```

```python
import functools

import jax
import jax.numpy as jnp
from jax import lax
from jax.experimental import pallas as pl
from jax.experimental.pallas import tpu as pltpu
from jax.sharding import PartitionSpec as P

DATES = 4
SETS = 64
LO = 256
LANES = 128
MESH = pl.DeviceIdType.MESH
BF = jnp.bfloat16
F32 = jnp.float32
NT = (((1,), (1,)), ((), ()))


def split3(x):
    a = x.astype(BF)
    r = x - a.astype(F32)
    b = r.astype(BF)
    c = (r - b.astype(F32)).astype(BF)
    return a, b, c


def kernel(
    nt,
    npath,
    coef_hbm,
    set_hbm,
    bkt_hbm,
    st_hbm,
    table_hbm,
    rw_hbm,
    corr_hbm,
    dw_hbm,
    out_ref,
    coef_ref,
    set_ref,
    bkt_ref,
    st_ref,
    table_ref,
    rw_ref,
    corr_ref,
    dw_ref,
    part,
    sens_out,
    sens_in,
    cell_in,
    hi_f,
    lo_f,
    s_f,
    acc,
    chi,
    cmid,
    clo,
    gradf,
    grad,
    tgp,
    tg,
    tg_in,
    msg,
    pr,
    st_out,
    st_in,
    load_sem,
    sens_ss,
    sens_rs,
    cell_ss,
    cell_rs,
    tg_ss,
    tg_rs,
    st_ss,
    st_rs,
    sib_ss,
    sib_rs,
    pr_ss,
    pr_rs,
):
    me = lax.axis_index("trade")
    mp = lax.axis_index("path")
    core = lax.rem(mp, 2)
    chip = mp // 2
    nchip = npath // 2
    rows = set_ref.shape[0]
    half = rows // 2
    nb = corr_ref.shape[0]
    wide = chi.shape[0]
    hi_rows = grad.shape[0]
    tiles, per_row = wide // LANES, LO // LANES
    apart = SETS // per_row
    per_date = nt // DATES
    ring = nchip // 2
    quarter = ring // 2

    def device(r, other):
        path = mp + other * (1 - 2 * core)
        return {"trade": lax.rem(me + r, nt), "path": path}

    def along(k):
        return {"path": lax.rem(chip + k, nchip) * 2 + core}

    loads = [
        pltpu.make_async_copy(src, dst, load_sem.at[i])
        for i, (src, dst) in enumerate(
            [
                (set_hbm, set_ref),
                (bkt_hbm, bkt_ref),
                (st_hbm, st_ref),
                (table_hbm, table_ref),
            ]
            + [(coef_hbm.at[d], coef_ref.at[d]) for d in range(DATES)]
            + [
                (corr_hbm, corr_ref),
                (rw_hbm, rw_ref),
                (dw_hbm, dw_ref),
            ]
        )
    ]
    for load in loads:
        load.start()

    barrier = pltpu.get_barrier_semaphore()
    for r in range(nt):
        for other in range(2):
            if r or other:
                pl.semaphore_signal(
                    barrier, inc=1, device_id=device(r, other), device_id_type=MESH
                )

    def greet(k, c):
        pl.semaphore_signal(barrier, inc=1, device_id=along(k), device_id_type=MESH)
        return c

    lax.fori_loop(1, nchip, greet, 0)

    def place(c):
        y, z, k = c // (2 * ring), c // 2 % ring, c % 2
        return ((z // quarter * 2 + k) * 2 + y) * quarter + z % quarter

    loads[0].wait()
    loads[1].wait()
    for c in range(rows):
        if c // 2 % quarter == 0:
            every = pl.ds(c, quarter, stride=2)
            cell_in[0, place(c) : place(c) + quarter, :] = (
                set_ref[every, :] * wide + bkt_ref[every, :]
            )

    def trade_copies(r):
        return (
            pltpu.make_async_remote_copy(
                src_ref=cell_in.at[0],
                dst_ref=cell_in.at[r],
                send_sem=cell_ss,
                recv_sem=cell_rs,
                device_id=device(r, 0),
                device_id_type=MESH,
            ),
            pltpu.make_async_remote_copy(
                src_ref=sens_out.at[lax.rem(me + r, nt)],
                dst_ref=sens_in.at[r],
                send_sem=sens_ss,
                recv_sem=sens_rs,
                device_id=device(r, 0),
                device_id_type=MESH,
            ),
        )

    far = sorted(range(nt), key=lambda r: -min(r, nt - r))

    loads[2].wait()
    loads[3].wait()
    lane = lax.broadcasted_iota(jnp.int32, table_ref.shape[1:], 1)
    for q in range(nt):
        d = q // per_date
        if q % per_date == 0:
            loads[4 + d].wait()
        state = st_ref[q % per_date, d]
        col = jnp.sum(jnp.where(lane == state, table_ref[d], 0.0), axis=1, keepdims=True)
        for c in range(rows):
            x = coef_ref[d, :, c * LANES : (c + 1) * LANES] * col
            at = place(c)
            part[at * 8 : (at + 1) * 8, :] = x[:8] + x[8:]
        tots = []
        for g in range(rows // 8):
            tot = part[pl.ds(g * 64, 8, stride=8), :]
            for s in range(1, 8):
                tot = tot + part[pl.ds(g * 64 + s, 8, stride=8), :]
            tots.append(tot)
        sens_out[q] = jnp.concatenate(tots, axis=0).astype(BF)

    pl.semaphore_wait(barrier, 2 * nt - 1 + nchip - 1)
    for i in range(2):
        for r in far[:-1]:
            trade_copies(r)[i].start()
    sens_in[0] = sens_out[me]

    for d in range(DATES):
        for p in range(per_date):
            q = d * per_date + p
            st_out[q : q + 1, :] = jnp.full((1, LANES), st_ref[p, d], jnp.int32).astype(F32)

    def send_state(k, c):
        pltpu.make_async_remote_copy(
            src_ref=st_out,
            dst_ref=st_in.at[core, chip],
            send_sem=st_ss,
            recv_sem=st_rs,
            device_id=along(k),
            device_id_type=MESH,
        ).start()
        return c

    lax.fori_loop(1, nchip, send_state, 0)
    st_in[core, chip] = st_out[...]
    others = pl.ds(0, nchip - 1)
    sibling = pltpu.make_async_remote_copy(
        src_ref=st_in.at[core],
        dst_ref=st_in.at[core],
        send_sem=sib_ss,
        recv_sem=sib_rs,
        device_id=device(0, 1),
        device_id_type=MESH,
    )

    loads[4 + DATES].wait()
    terms = (chi, cmid, clo)
    for ref, term in zip(terms, split3(corr_ref[...])):
        below, beside = nb // 16 * 16, nb // LANES * LANES
        ref[below:, :] = jnp.zeros((wide - below, wide), BF)
        ref[:, beside:] = jnp.zeros((wide, wide - beside), BF)
        ref[0:nb, 0:nb] = term

    hi_iota = lax.broadcasted_iota(jnp.int32, (hi_rows, LANES), 0).astype(F32).astype(BF)
    lo_iota = lax.broadcasted_iota(jnp.int32, (LO, LANES), 0).astype(F32).astype(BF)
    lo_lane = lax.broadcasted_iota(jnp.int32, (LANES, LO), 1).astype(F32).astype(BF)
    one, zero = jnp.ones((), BF), jnp.zeros((), BF)

    def spread(ref, row, n):
        x = jnp.broadcast_to(ref[pl.ds(row, 1), :], (16, LANES)).astype(BF)
        return jnp.broadcast_to(x[None], (n // 16, 16, LANES)).reshape(n, LANES)

    def unpack(src):
        base = src * rows
        cells = cell_in[src]
        h = lax.shift_right_logical(cells, 8)
        low = (cells - h * LO).astype(F32)
        hi_f[base : base + rows, :] = h.astype(F32)
        lo_f[base : base + rows, :] = low
        return low.T.astype(BF)

    def net_block(src, column):
        base = src * rows
        s_f[base : base + rows, :] = sens_in[src].astype(F32)
        left, right = [], []
        for i in range(rows):
            left.append(
                jnp.where(
                    spread(hi_f, base + i, hi_rows) == hi_iota, spread(s_f, base + i, hi_rows), zero
                )
            )
            right.append(
                jnp.where(
                    jnp.broadcast_to(column[:, i : i + 1], (LANES, LO)) == lo_lane, one, zero
                )
            )
        return jnp.dot(
            jnp.concatenate(left, axis=1),
            jnp.concatenate(right, axis=0),
            preferred_element_type=F32,
        )

    def halves(x):
        for k in range(per_row):
            acc[k] = x[:, k * LANES : (k + 1) * LANES]

    halves(net_block(0, unpack(0)))

    def wait_all(ref, sem):
        pltpu.make_async_copy(ref, ref, sem).wait()

    received = pl.ds(1, nt - 1)
    wait_all(cell_in.at[received], cell_rs)
    columns = [None] + [unpack(r) for r in range(1, nt)]
    wait_all(sens_in.at[received], sens_rs)

    total = jnp.concatenate([acc[k] for k in range(per_row)], axis=1)
    for r in range(1, nt):
        total = total + net_block(r, columns[r])
    halves(total)

    pltpu.make_async_copy(st_in.at[core, others], st_in.at[core, others], st_rs).wait()
    sibling.start()

    loads[5 + DATES].wait()
    loads[6 + DATES].wait()
    rw = jnp.concatenate(
        [rw_ref[...].reshape(1, nb), jnp.zeros((1, wide - nb), F32)], axis=1
    )
    def tile(rest, j):
        at = rest * tiles + j
        return at % per_row, pl.ds(at // per_row, apart, stride=tiles)

    def tile_of(ref, rest, j):
        half_row, every = tile(rest, j)
        return ref[half_row, every, :]

    netted = jnp.concatenate(
        [
            jnp.concatenate([tile_of(acc, rest, j) for j in range(tiles)], axis=1)
            for rest in range(per_row)
        ],
        axis=0,
    )
    w = netted * rw
    ws = split3(w)
    cw = jnp.zeros_like(w)
    for n in range(1, 4):
        stacked = jnp.dot(
            jnp.concatenate(ws[:n], axis=0), terms[3 - n][...], preferred_element_type=F32
        )
        for i in range(n - 1, -1, -1):
            cw = cw + stacked[i * SETS : (i + 1) * SETS]
    margin = jnp.sqrt(jnp.sum(w * cw, axis=1, keepdims=True) + 1.0)
    weight = dw_ref[me // per_date]
    net_grad = (weight * rw) * cw / margin
    for rest in range(per_row):
        for j in range(tiles):
            half_row, every = tile(rest, j)
            gradf[half_row, every, :] = net_grad[
                rest * apart : (rest + 1) * apart, j * LANES : (j + 1) * LANES
            ]
    grad[...] = jnp.concatenate([gradf[k] for k in range(per_row)], axis=1).astype(BF)

    def pick_blocks(dst, h, slot):
        def row(i):
            return pl.multiple_of(dst * rows + h * half, half) + i // half * rows + i % half

        right = jnp.concatenate(
            [
                jnp.where(spread(lo_f, row(i), LO) == lo_iota, one, zero)
                for i in range(rows)
            ],
            axis=1,
        )
        product = jnp.dot(grad[...], right, preferred_element_type=F32).astype(BF)
        for i in range(rows):
            kept = jnp.where(
                spread(hi_f, row(i), hi_rows) == hi_iota,
                product[:, i * LANES : (i + 1) * LANES],
                zero,
            ).reshape(hi_rows // 16, 16, LANES)
            tot = kept[0]
            for j in range(1, hi_rows // 16):
                tot = tot + kept[j]
            tot = tot.astype(F32)
            tgp[slot, i * 8 : (i + 1) * 8, :] = tot[:8] + tot[8:]
        for b in range(2):
            for k in range(2):
                at = (b * half + k * 8) * 8
                tot = tgp[slot, pl.ds(at, 8, stride=8), :]
                for s in range(1, 8):
                    tot = tot + tgp[slot, pl.ds(at + s, 8, stride=8), :]
                tg[dst + b, h, k] = tot

    def pick_copy(r, h, other):
        return pltpu.make_async_remote_copy(
            src_ref=tg.at[lax.rem(nt - r, nt), h, core + other * (1 - 2 * core)],
            dst_ref=tg_in.at[h, pl.ds(pl.multiple_of((core * nt + me) * 8, 8), 8)],
            send_sem=tg_ss.at[h],
            recv_sem=tg_rs.at[h],
            device_id=device(r, other),
            device_id_type=MESH,
        )

    def pick_step(n, c):
        h = n // 2
        first = (1 - lax.rem(n, 2)) * (nt // 2)
        pick_blocks(first + 2, h, 0)
        pick_blocks(first, h, 1)
        for b in range(nt // 2 - 1, 0, -1):
            for other in range(2):
                pick_copy(nt - first - b, h, other).start()
        pick_copy(lax.rem(nt - first, nt), h, 1).start()

        @pl.when(first > 0)
        def _():
            pick_copy(lax.rem(nt - first, nt), h, 0).start()

        return c

    lax.fori_loop(0, 4, pick_step, 0)

    mine = pl.ds(pl.multiple_of((core * nt + me) * 8, 8), 8)
    for h in range(2):
        tg_in[h, mine, :] = tg[0, h, core]

    def send_grad(target):
        return pltpu.make_async_remote_copy(
            src_ref=msg.at[target],
            dst_ref=pr.at[chip],
            send_sem=pr_ss,
            recv_sem=pr_rs,
            device_id={"path": target * 2 + core},
            device_id_type=MESH,
        )

    y, z = chip // ring, lax.rem(chip, ring)
    for h in range(2):
        wait_all(tg_in.at[h, pl.ds(0, (2 * nt - 1) * 8)], tg_rs.at[h])
        for c in range(half // 2):
            msg[c // quarter * ring + h * quarter + c % quarter] = jnp.concatenate(
                [tg_in[h, pl.ds(k * nt * 8 + c, nt, stride=8), :] for k in range(2)], axis=0
            ).astype(BF)
        for k in range(half // 2 - 1, 0, -1):
            to_z = h * quarter + lax.rem(z + k, quarter)
            send_grad(lax.rem(y + k // quarter, 2) * ring + to_z).start()
        same = y * ring + h * quarter + lax.rem(z, quarter)

        @pl.when(same != chip)
        def _():
            send_grad(same).start()

    pr[chip] = msg[chip]

    sibling.wait_recv()
    pairs = npath * nt
    ks = table_ref.shape[1]
    states = jnp.concatenate([st_in[k, c] for c in range(nchip) for k in range(2)], axis=0)
    hot = jnp.where(
        states == lax.broadcasted_iota(jnp.int32, (pairs, LANES), 1).astype(F32), 1.0, 0.0
    ).astype(BF)
    tab = jnp.concatenate(split3(table_ref[...].reshape(DATES * ks, LANES)), axis=0)
    at_date = lax.rem(
        lax.broadcasted_iota(jnp.int32, (3 * DATES * ks, pairs), 0) // ks, DATES
    )
    pair_date = lax.rem(
        lax.broadcasted_iota(jnp.int32, (3 * DATES * ks, pairs), 1), nt
    ) // per_date
    basis = jnp.where(
        at_date == pair_date, lax.dot_general(tab, hot, NT, preferred_element_type=F32), 0.0
    ).astype(BF)

    wait_all(cell_in.at[received], cell_ss)
    wait_all(sens_in.at[received], sens_ss)
    wait_all(tg_in.at[0, pl.ds(0, (2 * nt - 1) * 8)], tg_ss.at[0])
    wait_all(tg_in.at[1, pl.ds(0, (2 * nt - 1) * 8)], tg_ss.at[1])
    sibling.wait_send()
    pltpu.make_async_copy(st_in.at[core, others], st_in.at[core, others], st_ss).wait()
    pltpu.make_async_copy(pr.at[others], pr.at[others], pr_rs).wait()
    total = jnp.dot(basis, pr[...].reshape(pairs, LANES), preferred_element_type=F32)
    total = total.reshape(3, DATES, ks, LANES)
    out_ref[...] = total[0] + total[1] + total[2]

    pltpu.make_async_copy(pr.at[others], pr.at[others], pr_ss).wait()


def per_device(coef, set_ids, bucket_ids, states, table, risk_weight, correlation, date_weight):
    nt = lax.axis_size("trade")
    npath = lax.axis_size("path")
    trades = coef.shape[2]
    rows = trades // LANES
    nb = correlation.shape[0]
    wide = -(-nb // LANES) * LANES
    hi_rows = SETS * wide // LO
    ks = table.shape[1]
    vmem = pl.BlockSpec(memory_space=pltpu.VMEM)
    hbm = pl.BlockSpec(memory_space=pltpu.HBM)
    dma = pltpu.SemaphoreType.DMA
    return pl.pallas_call(
        functools.partial(kernel, nt, npath),
        out_shape=pltpu.VMEM((DATES, ks, LANES), F32),
        in_specs=[hbm] * 8,
        out_specs=vmem,
        scratch_shapes=[
            pltpu.VMEM(coef.shape, F32),
            pltpu.VMEM((rows, LANES), jnp.int32),
            pltpu.VMEM((rows, LANES), jnp.int32),
            pltpu.SMEM(states.shape[::-1], jnp.int32),
            pltpu.VMEM(table.shape, F32),
            pltpu.VMEM((nb,), F32),
            pltpu.VMEM(correlation.shape, F32),
            pltpu.SMEM(date_weight.shape, F32),
            pltpu.VMEM((rows * 8, LANES), F32),
            pltpu.VMEM((nt, rows, LANES), BF),
            pltpu.VMEM((nt, rows, LANES), BF),
            pltpu.VMEM((nt, rows, LANES), jnp.int32),
            pltpu.VMEM((nt * rows, LANES), F32),
            pltpu.VMEM((nt * rows, LANES), F32),
            pltpu.VMEM((nt * rows, LANES), F32),
            pltpu.VMEM((LO // LANES, hi_rows, LANES), F32),
            pltpu.VMEM((wide, wide), BF),
            pltpu.VMEM((wide, wide), BF),
            pltpu.VMEM((wide, wide), BF),
            pltpu.VMEM((LO // LANES, hi_rows, LANES), F32),
            pltpu.VMEM((hi_rows, LO), BF),
            pltpu.VMEM((2, rows * 8, LANES), F32),
            pltpu.VMEM((nt, 2, 2, 8, LANES), F32),
            pltpu.VMEM((2, 2 * nt * 8, LANES), F32),
            pltpu.VMEM((npath // 2, 2 * nt, LANES), BF),
            pltpu.VMEM((npath // 2, 2 * nt, LANES), BF),
            pltpu.VMEM((nt, LANES), F32),
            pltpu.VMEM((2, npath // 2, nt, LANES), F32),
            dma((7 + DATES,)),
            dma,
            dma,
            dma,
            dma,
            dma((2,)),
            dma((2,)),
            dma,
            dma,
            dma,
            dma,
            dma,
            dma,
        ],
        compiler_params=pltpu.CompilerParams(
            collective_id=0, has_side_effects=True, vmem_limit_bytes=48 * 1024 * 1024
        ),
    )(
        *(
            pltpu.with_memory_space_constraint(x, pltpu.HBM)
            for x in (
                coef,
                set_ids.reshape(rows, LANES),
                bucket_ids.reshape(rows, LANES),
                states.T,
                table,
                risk_weight,
                correlation,
                date_weight,
            )
        )
    )


def solution(mesh):
    in_specs = (P(None, None, "trade"), P("trade"), P("trade"), P(None, "path"), P(), P(), P(), P())
    out_specs = P(None, None, ("trade", "path"))
    return jax.shard_map(
        per_device, mesh=mesh, in_specs=in_specs, out_specs=out_specs, check_vma=False
    )
```
